256 devices in a mesh: dp: 2 (over core), ctx: 16 (over y, x), tp: 8 (over z).
Axes of the slice: x: 4, y: 4, z: 8, core: 2. Of those that a mesh axis runs over, the one named last changes fastest.
Arguments:
- queries: bfloat16 [2, 8192, 8192], P('dp', 'ctx', 'tp'), may hold values from -120 to 120
- keys: bfloat16 [2, 8192, 8192], P('dp', 'ctx', 'tp'), may hold values from -0.5 to 0.5
- values: bfloat16 [2, 8192, 8192], P('dp', 'ctx', 'tp'), may hold values from -180 to 180
- gate: bfloat16 [2, 8192, 8192], P('dp', 'ctx', 'tp'), may hold values from -8 to 8
- cotangent: bfloat16 [2, 8192, 8192], P('dp', 'ctx', 'tp'), may hold values from -6 to 6
- gain: float32 [8192], P('tp'), may hold values from 0.1 to 1.9
- slopes: float32 [64], P('tp'), may hold values from 1.2207031e-06 to 0.06
Outputs:
- query_gradient: bfloat16 [2, 8192, 8192], P('dp', 'ctx', 'tp')
- key_gradient: bfloat16 [2, 8192, 8192], P('dp', 'ctx', 'tp')
- grad_value: bfloat16 [2, 8192, 8192], P('dp', 'ctx', 'tp')
- grad_gate: bfloat16 [2, 8192, 8192], P('dp', 'ctx', 'tp')
- grad_gain: float32 [8192], P('tp')
The draws below stay inside these ranges and needn't reach their ends.
All inputs are finite; a program needn't handle non-finite values.
Results may differ from the reference program's by a relative error of at most 0.0062.
Values sent between devices are 32-bit elements; how exact they have to be, the bound alone decides.
A program may use at most 128 MiB of HBM per device.

```python
import math
import jax
import jax.numpy as jnp
from jax import lax

HEADS = 64
HD = 128
BLOCK = 512
BATCH = 2
SEQ = 8192
FEATURES = 8192


def draw_queries(key, part):
    key = jax.random.fold_in(key, 11)
    noise_key, row_key = jax.random.split(key)
    noise = jnp.clip(jax.random.normal(noise_key, (BATCH, SEQ, FEATURES), jnp.float32), -6.0, 6.0)
    extent = math.log(10.0)
    row_scale = jnp.exp(jax.random.uniform(row_key, (BATCH, SEQ, 1), jnp.float32, 0.0, extent))
    return (noise * row_scale).astype(jnp.bfloat16)


def draw_values(key, part):
    key = jax.random.fold_in(key, 23)
    noise_key, head_key = jax.random.split(key)
    noise = jnp.clip(jax.random.normal(noise_key, (BATCH, SEQ, HEADS, HD), jnp.float32), -6.0, 6.0)
    extent = math.log(10.0)
    head_index = jnp.arange(HEADS).astype(jnp.float32)
    jitter = jax.random.uniform(head_key, (HEADS,), jnp.float32, 0.0, 1.0)
    head_scale = jnp.exp(extent * (head_index + jitter) / HEADS)
    return (noise * head_scale[:, None]).reshape(BATCH, SEQ, FEATURES).astype(jnp.bfloat16)


def level_of(rng, shape, shards, low, largest):
    factor_of, own = 1.0, jax.random.fold_in(rng, 6)
    for dim, parts in shards:
        steps = jnp.exp(jax.random.uniform(jax.random.fold_in(own, dim), (parts,), jnp.float32, low / len(shards), largest / len(shards)))
        factor_of = factor_of * jnp.repeat(steps, shape[dim] // parts).reshape([-1 if axis == dim else 1 for axis in range(len(shape))])
    return factor_of


def gaussian(own_key, shape, width, limit, shards=(), kind=jnp.bfloat16):
    level = level_of(own_key, shape, shards, -0.22, 0.18) if shards else 1.0
    result = jax.random.normal(own_key, shape, jnp.float32) * width * level
    return jnp.minimum(jnp.maximum(result, -limit), limit).astype(kind)


def setup_inputs(seed: int = 0) -> dict:
    streams_of = jax.random.split(jax.random.key(seed), 8)
    queries = draw_queries(jax.random.fold_in(streams_of[7], 71), 0)
    keys = gaussian(streams_of[1], (BATCH, SEQ, FEATURES), HD ** -0.5, 0.5, ((0, 2), (1, 16), (2, 8)))
    values = draw_values(jax.random.fold_in(streams_of[7], 71), 0)
    gate = gaussian(streams_of[3], (BATCH, SEQ, FEATURES), 2.0, 8.0, ((0, 2), (1, 16), (2, 8)))
    cotangent = gaussian(streams_of[4], (BATCH, SEQ, FEATURES), 1.0, 6.0, ((0, 2), (1, 16), (2, 8)))
    gain = jnp.clip(1.0 + 0.18 * jax.random.normal(streams_of[5], (FEATURES,), jnp.float32), 0.1, 1.9)
    slopes = jnp.clip(jnp.exp(math.log(0.06) - 10.8026728 * jax.random.uniform(streams_of[6], (HEADS,), jnp.float32) ** level_of(streams_of[6], (HEADS,), ((0, 8),), -0.2, 0.2)), 1.220703097715159e-06, 0.06)
    return {"queries": queries, "keys": keys, "values": values, "gate": gate, "cotangent": cotangent, "gain": gain, "slopes": slopes}


EPSILON = 1e-05

def settle_state(values_in):
    return lax.optimization_barrier(values_in.astype(jnp.bfloat16)).astype(jnp.float32)

def tables(slopes):
    offsets = jnp.arange(BLOCK).astype(jnp.float32)
    distance = offsets[:, None] - offsets[None, :]
    decays = slopes[:, None, None]
    within_block = jnp.where(distance[None] >= 0.0, jnp.exp(-decays * jnp.maximum(distance, 0.0)[None]), 0.0)
    after = jnp.exp(-slopes[:, None] * (offsets[None, :] + 1.0))
    before = jnp.exp(-slopes[:, None] * (BLOCK - 1.0 - offsets[None, :]))
    whole = jnp.exp(-slopes * BLOCK)
    return (within_block, after, before, whole)

def reference(queries, keys, values, gate, cotangent, gain, slopes):
    within_block, after, before, whole = tables(slopes)
    number_blocks = SEQ // BLOCK
    leading_factor = after.T[:, :, None]
    trailing_factor = before.T[:, :, None]
    fading = whole[:, None, None]

    def blocked(array_in):
        return array_in.astype(jnp.float32).reshape(number_blocks, BLOCK, HEADS, HD)

    def sequence(bundle):
        query_row, key_row, value_row, gate_row, cot_row = bundle
        query_blocks = blocked(query_row)
        key_blocks = blocked(key_row)
        value_blocks = blocked(value_row)

        def forward(carried, block_in):
            block_of_queries, block_of_keys, block_of_values = block_in
            masked_scores = settle_state(jnp.einsum('xec,oec->exo', block_of_queries, block_of_keys) * within_block)
            memory_state = settle_state(carried)
            attended = jnp.einsum('hlm,mhe->lhe', masked_scores, block_of_values) + jnp.einsum('lhd,hde->lhe', block_of_queries, memory_state) * leading_factor
            keys_scaled = settle_state(block_of_keys * trailing_factor)
            carried = fading * carried + jnp.einsum('lhd,lhe->hde', keys_scaled, block_of_values)
            return (carried, (attended, memory_state))
        initial = jnp.zeros((HEADS, HD, HD), jnp.float32)
        _, (attended, memories) = lax.scan(forward, initial, (query_blocks, key_blocks, value_blocks))
        flattened = attended.reshape(SEQ, FEATURES)
        gated = jax.nn.sigmoid(gate_row.astype(jnp.float32))
        upstream = cot_row.astype(jnp.float32)
        grad_normed = upstream * gated
        scaled = grad_normed * gain
        square_sum = lax.optimization_barrier(jnp.sum(flattened * flattened, axis=1))
        cross_sum = lax.optimization_barrier(jnp.sum(scaled * flattened, axis=1))
        radius = lax.rsqrt(square_sum / FEATURES + EPSILON)[:, None]
        grad_gate = (upstream * flattened * radius * gain * gated * (1.0 - gated)).astype(jnp.bfloat16)
        gain_part = lax.optimization_barrier(jnp.sum(grad_normed * flattened * radius, axis=0))
        grad_attended = settle_state(radius * scaled - radius ** 3 * flattened * cross_sum[:, None] / FEATURES)
        grad_blocks = grad_attended.reshape(number_blocks, BLOCK, HEADS, HD)

        def backward(carried, block_in):
            block_of_queries, block_of_keys, block_of_values, block_gradient, memory_state = block_in
            masked_scores = settle_state(jnp.einsum('xec,oec->exo', block_of_queries, block_of_keys) * within_block)
            masked_scores_gradient = settle_state(jnp.einsum('lhe,mhe->hlm', block_gradient, block_of_values) * within_block)
            recalled_output = settle_state(carried)
            query_gradient = jnp.einsum('bqw,wbi->qbi', masked_scores_gradient, block_of_keys) + jnp.einsum('trz,rvz->trv', block_gradient, memory_state) * leading_factor
            key_gradient = jnp.einsum('guw,ugr->wgr', masked_scores_gradient, block_of_queries) + jnp.einsum('trz,rvz->trv', block_of_values, recalled_output) * trailing_factor
            grad_value = jnp.einsum('hlm,lhe->mhe', masked_scores, block_gradient) + jnp.einsum('lhd,hde->lhe', block_of_keys, recalled_output) * trailing_factor
            queries_scaled = settle_state(block_of_queries * leading_factor)
            carried = fading * carried + jnp.einsum('lhd,lhe->hde', queries_scaled, block_gradient)
            return (carried, (query_gradient.astype(jnp.bfloat16), key_gradient.astype(jnp.bfloat16), grad_value.astype(jnp.bfloat16)))
        _, (query_gradient, key_gradient, grad_value) = lax.scan(backward, initial, (query_blocks, key_blocks, value_blocks, grad_blocks, memories), reverse=True)
        return (query_gradient.reshape(SEQ, FEATURES), key_gradient.reshape(SEQ, FEATURES), grad_value.reshape(SEQ, FEATURES), grad_gate, gain_part)
    results = lax.map(sequence, (queries, keys, values, gate, cotangent))
    return (results[0], results[1], results[2], results[3], lax.optimization_barrier(jnp.sum(results[4], axis=0)))
```

```python
import functools

import jax
import jax.numpy as jnp
from jax import lax
from jax.experimental import pallas as pl
from jax.experimental.pallas import tpu as pltpu
from jax.sharding import PartitionSpec as P

HD = 128
BLOCK = 512
FEATURES = 8192
HEADS_HERE = 8
HALF = BLOCK // 2
CTX_X = 4
CTX_Y = 4
CTX = CTX_X * CTX_Y
TP = 8
CHUNKS = 4
PER = HEADS_HERE // CHUNKS
PART = HD // CTX
ROWS = PER * PART
EPSILON = 1e-05
MESH = pl.DeviceIdType.MESH

F32 = jnp.float32
BF16 = jnp.bfloat16

OFFSETS = sorted(
    [(dx, dy) for dx in range(CTX_X) for dy in range(CTX_Y) if (dx, dy) != (0, 0)],
    key=lambda o: -(min(o[0], CTX_X - o[0]) + min(o[1], CTX_Y - o[1])),
)
TP_OFFSETS = (4, 3, 5, 2, 6, 1, 7)

NN = (((1,), (0,)), ((), ()))
NT = (((1,), (1,)), ((), ()))
TN = (((0,), (0,)), ((), ()))


def dot(a, b, dims):
    return lax.dot_general(a, b, dims, preferred_element_type=F32)


def kernel(
    slopes, q_in, k_in, v_in, g_in, c_in, gain_ref,
    dq_out, dk_out, dv_out, dg_out, gain_out,
    q, k, v, g, c, dq, dk, dv, dg,
    after, before, masked, w_near, w_far, att, nrm, omg, qst, ga, mem, gm, dki, dvi,
    sq, cr, rcol, ccol,
    u, r1, s2, r2, zsend, zrecv, gsend, gpart, gboth, grecv,
    load_sem, out_sem, send1, recv1, send2, recv2, zs_sem, zr_sem, g_sem,
):
    me = lax.axis_index("ctx")
    me_x, me_y = lax.rem(me, CTX_X), lax.div(me, CTX_X)
    my_tp = lax.axis_index("tp")
    my_dp = lax.axis_index("dp")
    ctx_peers = [
        lax.rem(me_y + dy, CTX_Y) * CTX_X + lax.rem(me_x + dx, CTX_X) for dx, dy in OFFSETS
    ]
    tp_peers = [lax.rem(my_tp + o, TP) for o in TP_OFFSETS]
    partner = 1 - my_dp

    def load(n, src, dst, h):
        return pltpu.make_async_copy(
            src.at[0, :, pl.ds(pl.multiple_of(h * HD, HD), HD)], dst.at[h], load_sem.at[n, h]
        )

    def store(n, src, dst, h):
        return pltpu.make_async_copy(
            src.at[h], dst.at[0, :, pl.ds(pl.multiple_of(h * HD, HD), HD)], out_sem.at[n, h]
        )

    def load_kv(h, _):
        load(1, k_in, k, h).start()
        load(2, v_in, v, h).start()
        return 0

    def load_rest(h, _):
        load(0, q_in, q, h).start()
        load(3, g_in, g, h).start()
        load(4, c_in, c, h).start()
        return 0

    lax.fori_loop(0, HEADS_HERE, load_kv, 0)
    barrier = pltpu.get_barrier_semaphore()
    for p in ctx_peers:
        pl.semaphore_signal(barrier, inc=1, device_id={"ctx": p}, device_id_type=MESH)
    for p in tp_peers:
        pl.semaphore_signal(barrier, inc=1, device_id={"tp": p}, device_id_type=MESH)
    pl.semaphore_signal(barrier, inc=1, device_id={"dp": partner}, device_id_type=MESH)
    lax.fori_loop(0, HEADS_HERE, load_rest, 0)

    position = lax.broadcasted_iota(jnp.int32, (BLOCK, HD), 0).astype(F32)

    def exchange(src, dst, send, recv, n, p):
        return pltpu.make_async_remote_copy(
            src_ref=src.at[n, p],
            dst_ref=dst.at[n, me],
            send_sem=send.at[n],
            recv_sem=recv.at[n],
            device_id={"ctx": p},
            device_id_type=MESH,
        )

    def send_all(src, dst, send, recv, n):
        for p in ctx_peers:
            exchange(src, dst, send, recv, n, p).start()
        dst[n, me] = src[n, me]

    def waiter(src, dst, send, recv, n):
        return pltpu.make_async_remote_copy(
            src_ref=src.at[n, pl.ds(0, CTX - 1)],
            dst_ref=dst.at[n, pl.ds(0, CTX - 1)],
            send_sem=send.at[n],
            recv_sem=recv.at[n],
            device_id={"ctx": ctx_peers[0]},
            device_id_type=MESH,
        )

    def scan(d, n, reverse):
        waiter(u.at[d], r1.at[d], send1.at[d], recv1.at[d], n).wait_recv()
        fade = jnp.concatenate(
            [
                jnp.exp(jnp.full((PART, HD), -slopes[n * PER + i] * BLOCK, F32))
                for i in range(PER)
            ],
            axis=0,
        )
        total = jnp.zeros((ROWS, HD), F32)
        for b in reversed(range(CTX)) if reverse else range(CTX):
            s2[d, n, b] = total
            total = fade * total + r1[d, n, b]
        send_all(s2.at[d], r2.at[d], send2.at[d], recv2.at[d], n)

    def state(d, n, i):
        return r2[d, n, :, i * PART : (i + 1) * PART, :].reshape(HD, HD).astype(BF16)

    def put(d, n, i, value):
        u[d, n, :, i * PART : (i + 1) * PART, :] = value.reshape(CTX, PART, HD)

    def summary(n):
        for i in range(PER):
            h = n * PER + i
            load(1, k_in, k, h).wait()
            load(2, v_in, v, h).wait()
            weight = jnp.exp(-slopes[h] * (BLOCK - 1.0 - position))
            before[h] = weight
            scaled_keys = (k[h].astype(F32) * weight).astype(BF16)
            put(0, n, i, dot(scaled_keys, v[h], TN))

    def first(n, _):
        summary(n)
        send_all(u.at[0], r1.at[0], send1.at[0], recv1.at[0], n)
        return 0

    summary(0)
    pl.semaphore_wait(barrier, CTX - 1 + TP - 1 + 1)
    send_all(u.at[0], r1.at[0], send1.at[0], recv1.at[0], 0)
    lax.fori_loop(1, CHUNKS, first, 0)

    distance = (
        lax.broadcasted_iota(jnp.int32, (HALF, HALF), 0)
        - lax.broadcasted_iota(jnp.int32, (HALF, HALF), 1)
    ).astype(F32)

    def inside(h, _):
        load(0, q_in, q, h).wait()
        load(3, g_in, g, h).wait()
        load(4, c_in, c, h).wait()
        rate = slopes[h]
        near = jnp.where(distance >= 0.0, jnp.exp(-rate * jnp.maximum(distance, 0.0)), 0.0)
        far = jnp.exp(-rate * (distance + HALF))
        w_near[h] = near
        w_far[h] = far
        top, bottom = q[h, :HALF], q[h, HALF:]
        k_top, k_bottom = k[h, :HALF], k[h, HALF:]
        masked[h, 0] = (dot(top, k_top, NT) * near).astype(BF16)
        masked[h, 1] = (dot(bottom, k_top, NT) * far).astype(BF16)
        masked[h, 2] = (dot(bottom, k_bottom, NT) * near).astype(BF16)
        att[h, :HALF] = dot(masked[h, 0], v[h, :HALF], NN)
        att[h, HALF:] = dot(masked[h, 1], v[h, :HALF], NN) + dot(masked[h, 2], v[h, HALF:], NN)
        weight = jnp.exp(-rate * (position + 1.0))
        after[h] = weight
        qst[h] = (q[h].astype(F32) * weight).astype(BF16).T
        gated = 1.0 / (1.0 + jnp.exp(-g[h].astype(F32)))
        nrm[h] = c[h].astype(F32) * gated
        omg[h] = 1.0 - gated
        return 0

    def scan_forward(n, _):
        scan(0, n, False)
        return 0

    lax.fori_loop(0, HEADS_HERE // 2, inside, 0)
    lax.fori_loop(0, CHUNKS, scan_forward, 0)
    lax.fori_loop(HEADS_HERE // 2, HEADS_HERE, inside, 0)

    sq[...] = jnp.zeros_like(sq)
    cr[...] = jnp.zeros_like(cr)

    def attend(n, _):
        waiter(s2.at[0], r2.at[0], send2.at[0], recv2.at[0], n).wait_recv()
        for i in range(PER):
            h = n * PER + i
            memory = state(0, n, i)
            mem[h] = memory
            attended = att[h] + after[h] * dot(q[h], memory, NN)
            att[h] = attended
            sq[...] += attended * attended
            cr[...] += nrm[h] * gain_ref[pl.ds(h, 1), :] * attended
        return 0

    lax.fori_loop(0, CHUNKS, attend, 0)
    rows = [
        jnp.sum(ref[t * HD : (t + 1) * HD, :].T, axis=0, keepdims=True)
        for ref in (sq, cr)
        for t in range(BLOCK // HD)
    ]
    zsend[...] = jnp.concatenate(rows, axis=0)

    def tp_copy(i):
        return pltpu.make_async_remote_copy(
            src_ref=zsend,
            dst_ref=zrecv.at[my_tp],
            send_sem=zs_sem.at[i],
            recv_sem=zr_sem.at[i],
            device_id={"tp": tp_peers[i]},
            device_id_type=MESH,
        )

    for i in range(TP - 1):
        tp_copy(i).start()
    zrecv[my_tp] = zsend[...]
    for i in range(TP - 1):
        tp_copy(i).wait_recv()
    totals = zrecv[0]
    for i in range(1, TP):
        totals = totals + zrecv[i]
    radius = lax.rsqrt(totals[:4] / FEATURES + EPSILON)
    cross = radius * radius * radius * totals[4:] / FEATURES
    for t in range(BLOCK // HD):
        rows_here = pl.ds(t * HD, HD)
        rcol[rows_here, :] = jnp.broadcast_to(radius[t : t + 1], (HD, HD)).T
        ccol[rows_here, :] = jnp.broadcast_to(cross[t : t + 1], (HD, HD)).T

    def second(n, _):
        for i in range(PER):
            h = n * PER + i
            scaled = nrm[h] * gain_ref[pl.ds(h, 1), :]
            gradient = (rcol[...] * scaled - ccol[...] * att[h]).astype(BF16)
            ga[h] = gradient
            put(1, n, i, dot(qst[h], gradient, NN))
        send_all(u.at[1], r1.at[1], send1.at[1], recv1.at[1], n)
        return 0

    lax.fori_loop(0, CHUNKS, second, 0)

    def gate(h, _):
        common = nrm[h] * att[h] * rcol[...]
        gsend[pl.ds(h, 1), :] = jnp.sum(common, axis=0, keepdims=True)
        dg[h] = (common * gain_ref[pl.ds(h, 1), :] * omg[h]).astype(BF16)
        store(3, dg, dg_out, h).start()
        return 0

    lax.fori_loop(0, HEADS_HERE, gate, 0)
    pair = pltpu.make_async_remote_copy(
        src_ref=gsend,
        dst_ref=gpart,
        send_sem=g_sem.at[0],
        recv_sem=g_sem.at[1],
        device_id={"dp": partner},
        device_id_type=MESH,
    )
    pair.start()

    def backward(h, _):
        gradient = ga[h]
        g_top, g_bottom = ga[h, :HALF], ga[h, HALF:]
        v_top, v_bottom = v[h, :HALF], v[h, HALF:]
        near, far = w_near[h], w_far[h]
        m0 = (dot(g_top, v_top, NT) * near).astype(BF16)
        m1 = (dot(g_bottom, v_top, NT) * far).astype(BF16)
        m2 = (dot(g_bottom, v_bottom, NT) * near).astype(BF16)
        gm[0] = m0
        gm[1] = m1
        gm[2] = m2
        k_top, k_bottom = k[h, :HALF], k[h, HALF:]
        carried = after[h] * dot(gradient, mem[h], NT)
        dq[h, :HALF] = (dot(gm[0], k_top, NN) + carried[:HALF]).astype(BF16)
        dq[h, HALF:] = (
            dot(gm[1], k_top, NN) + dot(gm[2], k_bottom, NN) + carried[HALF:]
        ).astype(BF16)
        store(0, dq, dq_out, h).start()
        dki[h, :HALF] = dot(gm[0], q[h, :HALF], TN) + dot(gm[1], q[h, HALF:], TN)
        dki[h, HALF:] = dot(gm[2], q[h, HALF:], TN)
        dvi[h, :HALF] = dot(masked[h, 0], g_top, TN) + dot(masked[h, 1], g_bottom, TN)
        dvi[h, HALF:] = dot(masked[h, 2], g_bottom, TN)
        return 0

    def scan_backward(n, _):
        scan(1, n, True)
        return 0

    lax.fori_loop(0, HEADS_HERE // 4, backward, 0)
    pair.wait_recv()
    gboth[...] = gsend[...] + gpart[...]
    lax.fori_loop(0, CHUNKS, scan_backward, 0)

    def gain_copy(p):
        return pltpu.make_async_remote_copy(
            src_ref=gboth,
            dst_ref=grecv.at[me],
            send_sem=g_sem.at[2],
            recv_sem=g_sem.at[3],
            device_id={"ctx": p},
            device_id_type=MESH,
        )

    for p in ctx_peers:
        gain_copy(p).start()
    grecv[me] = gboth[...]
    lax.fori_loop(HEADS_HERE // 4, HEADS_HERE, backward, 0)

    def sent(n, _):
        waiter(u.at[0], r1.at[0], send1.at[0], recv1.at[0], n).wait_send()
        waiter(s2.at[0], r2.at[0], send2.at[0], recv2.at[0], n).wait_send()
        waiter(u.at[1], r1.at[1], send1.at[1], recv1.at[1], n).wait_send()
        return 0

    lax.fori_loop(0, CHUNKS, sent, 0)
    for i in range(TP - 1):
        tp_copy(i).wait_send()
    pair.wait_send()

    def finish(n, _):
        waiter(s2.at[1], r2.at[1], send2.at[1], recv2.at[1], n).wait_recv()
        for i in range(PER):
            h = n * PER + i
            recalled = state(1, n, i)
            dk[h] = (dki[h] + before[h] * dot(v[h], recalled, NT)).astype(BF16)
            store(1, dk, dk_out, h).start()
            dv[h] = (dvi[h] + before[h] * dot(k[h], recalled, NN)).astype(BF16)
            store(2, dv, dv_out, h).start()
        return 0

    lax.fori_loop(0, CHUNKS, finish, 0)

    gain_all = pltpu.make_async_remote_copy(
        src_ref=grecv.at[pl.ds(0, CTX - 1)],
        dst_ref=grecv.at[pl.ds(0, CTX - 1)],
        send_sem=g_sem.at[2],
        recv_sem=g_sem.at[3],
        device_id={"ctx": ctx_peers[0]},
        device_id_type=MESH,
    )
    gain_all.wait_recv()
    gain_all.wait_send()
    total = grecv[0]
    for i in range(1, CTX):
        total = total + grecv[i]
    gain_out[...] = total

    def drain(n, _):
        waiter(s2.at[1], r2.at[1], send2.at[1], recv2.at[1], n).wait_send()
        return 0

    def stored(h, _):
        store(0, dq, dq_out, h).wait()
        store(1, dk, dk_out, h).wait()
        store(2, dv, dv_out, h).wait()
        store(3, dg, dg_out, h).wait()
        return 0

    lax.fori_loop(0, CHUNKS, drain, 0)
    lax.fori_loop(0, HEADS_HERE, stored, 0)


def per_device(queries, keys, values, gate, cotangent, gain, slopes):
    whole = jax.ShapeDtypeStruct((1, BLOCK, HEADS_HERE * HD), BF16)
    heads16 = pltpu.VMEM((HEADS_HERE, BLOCK, HD), BF16)
    heads32 = pltpu.VMEM((HEADS_HERE, BLOCK, HD), F32)
    column = pltpu.VMEM((BLOCK, HD), F32)
    travel = pltpu.VMEM((2, CHUNKS, CTX, ROWS, HD), F32)
    tile = pltpu.VMEM((HEADS_HERE, HD), F32)
    dma = pltpu.SemaphoreType.DMA
    scratch = (
        [heads16] * 9
        + [
            heads32,
            heads32,
            pltpu.VMEM((HEADS_HERE, 3, HALF, HALF), BF16),
            pltpu.VMEM((HEADS_HERE, HALF, HALF), F32),
            pltpu.VMEM((HEADS_HERE, HALF, HALF), F32),
            heads32,
            heads32,
            heads32,
            pltpu.VMEM((HEADS_HERE, HD, BLOCK), BF16),
            heads16,
            pltpu.VMEM((HEADS_HERE, HD, HD), BF16),
            pltpu.VMEM((3, HALF, HALF), BF16),
            heads32,
            heads32,
        ]
        + [column] * 4
        + [travel] * 4
        + [
            tile,
            pltpu.VMEM((TP, 8, HD), F32),
            tile,
            tile,
            tile,
            pltpu.VMEM((CTX, HEADS_HERE, HD), F32),
            dma((5, HEADS_HERE)),
            dma((4, HEADS_HERE)),
        ]
        + [dma((2, CHUNKS))] * 4
        + [dma((TP - 1,)), dma((TP - 1,)), dma((4,))]
    )
    anywhere = pl.BlockSpec(memory_space=pl.ANY)
    in_vmem = pl.BlockSpec(memory_space=pltpu.VMEM)
    flops = HEADS_HERE * BLOCK * HD * 2 * (6 * BLOCK * 3 // 4 + 6 * HD)
    dq, dk, dv, dg, total = pl.pallas_call(
        kernel,
        out_shape=(whole, whole, whole, whole, jax.ShapeDtypeStruct((HEADS_HERE, HD), F32)),
        in_specs=[pl.BlockSpec(memory_space=pltpu.SMEM)] + [anywhere] * 5 + [in_vmem],
        out_specs=(anywhere, anywhere, anywhere, anywhere, in_vmem),
        scratch_shapes=scratch,
        compiler_params=pltpu.CompilerParams(
            collective_id=0, has_side_effects=True, vmem_limit_bytes=56 << 20
        ),
        cost_estimate=pl.CostEstimate(
            flops=flops, bytes_accessed=9 << 20, transcendentals=HEADS_HERE * BLOCK * BLOCK
        ),
        name="lightning_backward",
    )(slopes, queries, keys, values, gate, cotangent, gain.reshape(HEADS_HERE, HD))
    return dq, dk, dv, dg, total.reshape(HEADS_HERE * HD)


def solution(mesh):
    wide = P("dp", "ctx", "tp")
    return jax.shard_map(
        per_device,
        mesh=mesh,
        in_specs=(wide, wide, wide, wide, wide, P("tp"), P("tp")),
        out_specs=(wide, wide, wide, wide, P("tp")),
        check_vma=False,
    )
```

```python
import functools

import jax
import jax.numpy as jnp
from jax import lax
from jax.experimental import pallas as pl
from jax.experimental.pallas import tpu as pltpu
from jax.sharding import PartitionSpec as P

HD = 128
BLOCK = 512
FEATURES = 8192
HEADS_HERE = 8
HALF = BLOCK // 2
CTX_X = 4
CTX_Y = 4
CTX = CTX_X * CTX_Y
TP = 8
CHUNKS = 4
PER = HEADS_HERE // CHUNKS
PART = HD // CTX
PIECE = 512
ROWS = PER * PART
EPSILON = 1e-05
MESH = pl.DeviceIdType.MESH

F32 = jnp.float32
BF16 = jnp.bfloat16

OFFSETS = sorted(
    [(dx, dy) for dx in range(CTX_X) for dy in range(CTX_Y) if (dx, dy) != (0, 0)],
    key=lambda o: -(min(o[0], CTX_X - o[0]) + min(o[1], CTX_Y - o[1])),
)
TP_OFFSETS = (4, 3, 5, 2, 6, 1, 7)

NN = (((1,), (0,)), ((), ()))
NT = (((1,), (1,)), ((), ()))
TN = (((0,), (0,)), ((), ()))
TT = (((0,), (1,)), ((), ()))


def dot(a, b, dims):
    return lax.dot_general(a, b, dims, preferred_element_type=F32)


def kernel(
    slopes_in, q_in, k_in, v_in, g_in, c_in, gain_in,
    dq, dk, dv, dg, gain_out,
    slopes, gain_ref, q, k, v, g, c,
    after, before, masked, w_near, w_far, att_t, sca_t, nrm, omg, qst, ga_t, ga, mem, gm, dki, dvi,
    sums, stats, rcol,
    u, r1, s2, r2, zsend, zrecv, gsend, gpart, gboth, grecv,
    small_sem, load_sem, send1, recv1, send2, recv2, zs_sem, zr_sem, g_sem,
):
    me = lax.axis_index("ctx")
    me_x, me_y = lax.rem(me, CTX_X), lax.div(me, CTX_X)
    my_tp = lax.axis_index("tp")
    my_dp = lax.axis_index("dp")
    ctx_peers = [
        lax.rem(me_y + dy, CTX_Y) * CTX_X + lax.rem(me_x + dx, CTX_X) for dx, dy in OFFSETS
    ]
    tp_peers = [lax.rem(my_tp + o, TP) for o in TP_OFFSETS]
    partner = 1 - my_dp

    def load(n, src, dst, h):
        return pltpu.make_async_copy(
            src.at[0, :, pl.ds(pl.multiple_of(h * HD, HD), HD)], dst.at[h], load_sem.at[n, h]
        )

    def load_kv(h, _):
        load(1, k_in, k, h).start()
        load(2, v_in, v, h).start()
        return 0

    def load_rest(h, _):
        load(0, q_in, q, h).start()
        load(3, g_in, g, h).start()
        load(4, c_in, c, h).start()
        return 0

    def lanes(h):
        return pl.ds(pl.multiple_of(h * HD, HD), HD)

    slopes_copy = pltpu.make_async_copy(slopes_in, slopes, small_sem.at[0])
    gain_copy_in = pltpu.make_async_copy(gain_in, gain_ref, small_sem.at[1])
    slopes_copy.start()
    lax.fori_loop(0, PER, load_kv, 0)
    barrier = pltpu.get_barrier_semaphore()
    for p in ctx_peers:
        pl.semaphore_signal(barrier, inc=1, device_id={"ctx": p}, device_id_type=MESH)
    for p in tp_peers:
        pl.semaphore_signal(barrier, inc=1, device_id={"tp": p}, device_id_type=MESH)
    pl.semaphore_signal(barrier, inc=1, device_id={"dp": partner}, device_id_type=MESH)
    lax.fori_loop(PER, HEADS_HERE, load_kv, 0)
    gain_copy_in.start()
    lax.fori_loop(0, HEADS_HERE, load_rest, 0)
    slopes_copy.wait()

    position = lax.broadcasted_iota(jnp.int32, (BLOCK, HD), 0).astype(F32)
    along = lax.broadcasted_iota(jnp.int32, (1, BLOCK), 1).astype(F32)

    def exchange(src, dst, send, recv, n, p):
        return pltpu.make_async_remote_copy(
            src_ref=src.at[n, p],
            dst_ref=dst.at[n, me],
            send_sem=send.at[n],
            recv_sem=recv.at[n],
            device_id={"ctx": p},
            device_id_type=MESH,
        )

    def send_all(src, dst, send, recv, n):
        for p in ctx_peers:
            exchange(src, dst, send, recv, n, p).start()
        dst[n, me] = src[n, me]

    def waiter(src, dst, send, recv, n):
        return pltpu.make_async_remote_copy(
            src_ref=src.at[n, pl.ds(0, CTX - 1)],
            dst_ref=dst.at[n, pl.ds(0, CTX - 1)],
            send_sem=send.at[n],
            recv_sem=recv.at[n],
            device_id={"ctx": ctx_peers[0]},
            device_id_type=MESH,
        )

    def scan(d, n, reverse):
        waiter(u.at[d], r1.at[d], send1.at[d], recv1.at[d], n).wait_recv()
        fade = jnp.concatenate(
            [
                jnp.exp(jnp.full((PART, HD), -slopes[n * PER + i] * BLOCK, F32))
                for i in range(PER)
            ],
            axis=0,
        )
        total = jnp.zeros((ROWS, HD), F32)
        for b in reversed(range(CTX)) if reverse else range(CTX):
            s2[d, n, b] = total
            total = fade * total + r1[d, n, b]
        send_all(s2.at[d], r2.at[d], send2.at[d], recv2.at[d], n)

    def state(d, n, i):
        return r2[d, n, :, i * PART : (i + 1) * PART, :].reshape(HD, HD).astype(BF16)

    def put(d, n, i, value):
        u[d, n, :, i * PART : (i + 1) * PART, :] = value.reshape(CTX, PART, HD)

    def summary(n):
        for i in range(PER):
            h = n * PER + i
            before[h] = jnp.exp(-slopes[h] * (BLOCK - 1.0 - position))
        for i in range(PER):
            h = n * PER + i
            load(1, k_in, k, h).wait()
            load(2, v_in, v, h).wait()
            scaled_keys = (k[h].astype(F32) * before[h]).astype(BF16)
            put(0, n, i, dot(scaled_keys, v[h], TN))

    def first(n, _):
        summary(n)
        send_all(u.at[0], r1.at[0], send1.at[0], recv1.at[0], n)
        return 0

    summary(0)
    pl.semaphore_wait(barrier, CTX - 1 + TP - 1 + 1)
    send_all(u.at[0], r1.at[0], send1.at[0], recv1.at[0], 0)
    lax.fori_loop(1, CHUNKS, first, 0)

    distance = (
        lax.broadcasted_iota(jnp.int32, (HALF, HALF), 0)
        - lax.broadcasted_iota(jnp.int32, (HALF, HALF), 1)
    ).astype(F32)

    def inside(h, _):
        load(0, q_in, q, h).wait()
        load(3, g_in, g, h).wait()
        load(4, c_in, c, h).wait()
        rate = slopes[h]
        near = jnp.where(distance >= 0.0, jnp.exp(-rate * jnp.maximum(distance, 0.0)), 0.0)
        far = jnp.exp(-rate * (distance + HALF))
        w_near[h] = near
        w_far[h] = far
        top, bottom = q[h, :HALF], q[h, HALF:]
        k_top, k_bottom = k[h, :HALF], k[h, HALF:]
        masked[h, 0] = (dot(top, k_top, NT) * near).astype(BF16)
        masked[h, 1] = (dot(bottom, k_top, NT) * far).astype(BF16)
        masked[h, 2] = (dot(bottom, k_bottom, NT) * near).astype(BF16)
        att_t[h, :, :HALF] = dot(masked[h, 0], v[h, :HALF], NN).T
        att_t[h, :, HALF:] = (
            dot(masked[h, 1], v[h, :HALF], NN) + dot(masked[h, 2], v[h, HALF:], NN)
        ).T
        weight = jnp.exp(-rate * (position + 1.0))
        after[h] = weight
        qst[h] = (q[h].astype(F32) * weight).astype(BF16).T
        gated = 1.0 / (1.0 + jnp.exp(-g[h].astype(F32)))
        normed = c[h].astype(F32) * gated
        nrm[h] = normed
        sca_t[h] = (normed * gain_ref[pl.ds(h, 1), :]).T
        omg[h] = 1.0 - gated
        return 0

    def scan_forward(n, _):
        scan(0, n, False)
        return 0

    gain_copy_in.wait()
    lax.fori_loop(0, HEADS_HERE // 2, inside, 0)
    lax.fori_loop(0, CHUNKS, scan_forward, 0)
    lax.fori_loop(HEADS_HERE // 2, HEADS_HERE, inside, 0)

    sums[...] = jnp.zeros_like(sums)

    def attend(n, _):
        waiter(s2.at[0], r2.at[0], send2.at[0], recv2.at[0], n).wait_recv()
        for i in range(PER):
            h = n * PER + i
            memory = state(0, n, i)
            mem[h] = memory
            fade = jnp.exp(-slopes[h] * (along + 1.0))
            attended = att_t[h] + fade * dot(memory, q[h], TT)
            att_t[h] = attended
            sums[0] += jnp.sum((attended * attended).reshape(HD // 8, 8, BLOCK), axis=0)
            sums[1] += jnp.sum((sca_t[h] * attended).reshape(HD // 8, 8, BLOCK), axis=0)
        return 0

    lax.fori_loop(0, CHUNKS, attend, 0)
    rows = []
    for n in range(2):
        row = jnp.sum(sums[n], axis=0, keepdims=True)
        rows += [row[:, t * HD : (t + 1) * HD] for t in range(BLOCK // HD)]
    zsend[...] = jnp.concatenate(rows, axis=0)

    def tp_copy(i):
        return pltpu.make_async_remote_copy(
            src_ref=zsend,
            dst_ref=zrecv.at[my_tp],
            send_sem=zs_sem.at[i],
            recv_sem=zr_sem.at[i],
            device_id={"tp": tp_peers[i]},
            device_id_type=MESH,
        )

    for i in range(TP - 1):
        tp_copy(i).start()
    zrecv[my_tp] = zsend[...]
    for i in range(TP - 1):
        tp_copy(i).wait_recv()
    totals = zrecv[0]
    for i in range(1, TP):
        totals = totals + zrecv[i]
    radius = lax.rsqrt(totals[:4] / FEATURES + EPSILON)
    cross = radius * radius * radius * totals[4:] / FEATURES
    stats[0] = jnp.concatenate([radius[t : t + 1] for t in range(4)], axis=1)
    stats[1] = jnp.concatenate([cross[t : t + 1] for t in range(4)], axis=1)

    def second(n, _):
        for i in range(PER):
            h = n * PER + i
            gradient = (stats[0] * sca_t[h] - stats[1] * att_t[h]).astype(BF16)
            ga_t[h] = gradient
            put(1, n, i, dot(qst[h], gradient, NT))
        send_all(u.at[1], r1.at[1], send1.at[1], recv1.at[1], n)
        return 0

    lax.fori_loop(0, CHUNKS, second, 0)

    for t in range(BLOCK // HD):
        column = stats[0, :, t * HD : (t + 1) * HD]
        rcol[t * HD : (t + 1) * HD, :] = jnp.broadcast_to(column, (HD, HD)).T

    def gate(h, _):
        ga[h] = ga_t[h].T
        common = nrm[h] * att_t[h].T * rcol[...]
        gsend[pl.ds(h, 1), :] = jnp.sum(common, axis=0, keepdims=True)
        dg[:, lanes(h)] = (common * gain_ref[pl.ds(h, 1), :] * omg[h]).astype(BF16)
        return 0

    lax.fori_loop(0, HEADS_HERE, gate, 0)
    pair = pltpu.make_async_remote_copy(
        src_ref=gsend,
        dst_ref=gpart,
        send_sem=g_sem.at[0],
        recv_sem=g_sem.at[1],
        device_id={"dp": partner},
        device_id_type=MESH,
    )
    pair.start()

    def backward(h, _):
        gradient = ga[h]
        g_top, g_bottom = ga[h, :HALF], ga[h, HALF:]
        v_top, v_bottom = v[h, :HALF], v[h, HALF:]
        near, far = w_near[h], w_far[h]
        m0 = (dot(g_top, v_top, NT) * near).astype(BF16)
        m1 = (dot(g_bottom, v_top, NT) * far).astype(BF16)
        m2 = (dot(g_bottom, v_bottom, NT) * near).astype(BF16)
        gm[0] = m0
        gm[1] = m1
        gm[2] = m2
        k_top, k_bottom = k[h, :HALF], k[h, HALF:]
        carried = after[h] * dot(gradient, mem[h], NT)
        dq[:HALF, lanes(h)] = (dot(gm[0], k_top, NN) + carried[:HALF]).astype(BF16)
        dq[HALF:, lanes(h)] = (
            dot(gm[1], k_top, NN) + dot(gm[2], k_bottom, NN) + carried[HALF:]
        ).astype(BF16)
        dki[h, :HALF] = dot(gm[0], q[h, :HALF], TN) + dot(gm[1], q[h, HALF:], TN)
        dki[h, HALF:] = dot(gm[2], q[h, HALF:], TN)
        dvi[h, :HALF] = dot(masked[h, 0], g_top, TN) + dot(masked[h, 1], g_bottom, TN)
        dvi[h, HALF:] = dot(masked[h, 2], g_bottom, TN)
        return 0

    def scan_backward(n, _):
        scan(1, n, True)
        return 0

    lax.fori_loop(0, HEADS_HERE // 4, backward, 0)
    pair.wait_recv()
    gboth[...] = gsend[...] + gpart[...]
    lax.fori_loop(0, CHUNKS, scan_backward, 0)

    def gain_copy(p):
        return pltpu.make_async_remote_copy(
            src_ref=gboth,
            dst_ref=grecv.at[me],
            send_sem=g_sem.at[2],
            recv_sem=g_sem.at[3],
            device_id={"ctx": p},
            device_id_type=MESH,
        )

    for p in ctx_peers:
        gain_copy(p).start()
    grecv[me] = gboth[...]
    lax.fori_loop(HEADS_HERE // 4, HEADS_HERE, backward, 0)

    def sent(n, _):
        waiter(u.at[0], r1.at[0], send1.at[0], recv1.at[0], n).wait_send()
        waiter(s2.at[0], r2.at[0], send2.at[0], recv2.at[0], n).wait_send()
        waiter(u.at[1], r1.at[1], send1.at[1], recv1.at[1], n).wait_send()
        return 0

    lax.fori_loop(0, CHUNKS, sent, 0)
    for i in range(TP - 1):
        tp_copy(i).wait_send()
    pair.wait_send()

    def finish(n, _):
        waiter(s2.at[1], r2.at[1], send2.at[1], recv2.at[1], n).wait_recv()
        for i in range(PER):
            h = n * PER + i
            recalled = state(1, n, i)
            dk[:, lanes(h)] = (dki[h] + before[h] * dot(v[h], recalled, NT)).astype(BF16)
            dv[:, lanes(h)] = (dvi[h] + before[h] * dot(k[h], recalled, NN)).astype(BF16)
        return 0

    lax.fori_loop(0, CHUNKS, finish, 0)

    gain_all = pltpu.make_async_remote_copy(
        src_ref=grecv.at[pl.ds(0, CTX - 1)],
        dst_ref=grecv.at[pl.ds(0, CTX - 1)],
        send_sem=g_sem.at[2],
        recv_sem=g_sem.at[3],
        device_id={"ctx": ctx_peers[0]},
        device_id_type=MESH,
    )
    gain_all.wait_recv()
    gain_all.wait_send()
    total = grecv[0]
    for i in range(1, CTX):
        total = total + grecv[i]
    gain_out[...] = total

    def drain(n, _):
        waiter(s2.at[1], r2.at[1], send2.at[1], recv2.at[1], n).wait_send()
        return 0

    lax.fori_loop(0, CHUNKS, drain, 0)


def place(dq_in, dk_in, dv_in, dg_in, gain_in, dq, dk, dv, dg, gain, sem):
    pairs = ((dq_in, dq), (dk_in, dk), (dv_in, dv), (dg_in, dg))
    copies = [
        pltpu.make_async_copy(
            src.at[pl.ds(i * PIECE, PIECE)], dst.at[0, pl.ds(i * PIECE, PIECE)], sem.at[n, i]
        )
        for i in range(BLOCK // PIECE)
        for n, (src, dst) in enumerate(pairs)
    ]
    for copy in copies:
        copy.start()
    gain[...] = gain_in[...]
    for copy in copies:
        copy.wait()


def per_device(queries, keys, values, gate, cotangent, gain, slopes):
    whole = jax.ShapeDtypeStruct((1, BLOCK, HEADS_HERE * HD), BF16)
    flat = pltpu.VMEM((BLOCK, HEADS_HERE * HD), BF16)
    heads16 = pltpu.VMEM((HEADS_HERE, BLOCK, HD), BF16)
    heads32 = pltpu.VMEM((HEADS_HERE, BLOCK, HD), F32)
    heads16_t = pltpu.VMEM((HEADS_HERE, HD, BLOCK), BF16)
    heads32_t = pltpu.VMEM((HEADS_HERE, HD, BLOCK), F32)
    travel = pltpu.VMEM((2, CHUNKS, CTX, ROWS, HD), F32)
    tile = pltpu.VMEM((HEADS_HERE, HD), F32)
    dma = pltpu.SemaphoreType.DMA
    scratch = (
        [pltpu.SMEM((HEADS_HERE,), F32), tile]
        + [heads16] * 5
        + [
            heads32,
            heads32,
            pltpu.VMEM((HEADS_HERE, 3, HALF, HALF), BF16),
            pltpu.VMEM((HEADS_HERE, HALF, HALF), F32),
            pltpu.VMEM((HEADS_HERE, HALF, HALF), F32),
            heads32_t,
            heads32_t,
            heads32,
            heads32,
            heads16_t,
            heads16_t,
            heads16,
            pltpu.VMEM((HEADS_HERE, HD, HD), BF16),
            pltpu.VMEM((3, HALF, HALF), BF16),
            heads32,
            heads32,
        ]
        + [
            pltpu.VMEM((2, 8, BLOCK), F32),
            pltpu.VMEM((2, 1, BLOCK), F32),
            pltpu.VMEM((BLOCK, HD), F32),
        ]
        + [travel] * 4
        + [
            tile,
            pltpu.VMEM((TP, 8, HD), F32),
            tile,
            tile,
            tile,
            pltpu.VMEM((CTX, HEADS_HERE, HD), F32),
            dma((2,)),
            dma((5, HEADS_HERE)),
        ]
        + [dma((2, CHUNKS))] * 4
        + [dma((TP - 1,)), dma((TP - 1,)), dma((4,))]
    )
    anywhere = pl.BlockSpec(memory_space=pl.ANY)
    in_hbm = pl.BlockSpec(memory_space=pltpu.HBM)
    in_vmem = pl.BlockSpec(memory_space=pltpu.VMEM)
    flops = HEADS_HERE * BLOCK * HD * 2 * (6 * BLOCK * 3 // 4 + 6 * HD)
    whole_inputs = [
        pltpu.with_memory_space_constraint(x, pltpu.HBM)
        for x in (
            slopes, queries, keys, values, gate, cotangent, gain.reshape(HEADS_HERE, HD)
        )
    ]
    results = pl.pallas_call(
        kernel,
        out_shape=(flat, flat, flat, flat, tile),
        in_specs=[in_hbm] * 7,
        out_specs=(in_vmem,) * 5,
        scratch_shapes=scratch,
        compiler_params=pltpu.CompilerParams(
            collective_id=0, has_side_effects=True, vmem_limit_bytes=44 << 20
        ),
        cost_estimate=pl.CostEstimate(
            flops=flops, bytes_accessed=5 << 20, transcendentals=HEADS_HERE * BLOCK * BLOCK
        ),
        name="lightning_backward",
    )(*whole_inputs)
    results = [pltpu.with_memory_space_constraint(x, pltpu.VMEM) for x in results]
    dq, dk, dv, dg, total = pl.pallas_call(
        place,
        out_shape=(whole, whole, whole, whole, jax.ShapeDtypeStruct((HEADS_HERE, HD), F32)),
        in_specs=[in_vmem] * 5,
        out_specs=(anywhere,) * 4 + (in_vmem,),
        scratch_shapes=[dma((4, BLOCK // PIECE))],
        compiler_params=pltpu.CompilerParams(vmem_limit_bytes=2 << 20),
        cost_estimate=pl.CostEstimate(flops=0, bytes_accessed=8 << 20, transcendentals=0),
        name="place_results",
    )(*results)
    return dq, dk, dv, dg, total.reshape(HEADS_HERE * HD)


def solution(mesh):
    wide = P("dp", "ctx", "tp")
    return jax.shard_map(
        per_device,
        mesh=mesh,
        in_specs=(wide, wide, wide, wide, wide, P("tp"), P("tp")),
        out_specs=(wide, wide, wide, wide, P("tp")),
        check_vma=False,
    )
```

```python
import functools

import jax
import jax.numpy as jnp
from jax import lax
from jax.experimental import pallas as pl
from jax.experimental.pallas import tpu as pltpu
from jax.sharding import PartitionSpec as P

HD = 128
BLOCK = 512
FEATURES = 8192
HEADS_HERE = 8
HALF = BLOCK // 2
CTX_X = 4
CTX_Y = 4
CTX = CTX_X * CTX_Y
TP = 8
CHUNKS = 4
PER = HEADS_HERE // CHUNKS
PART = HD // CTX
PIECE = 512
ROWS = PER * PART
EPSILON = 1e-05
MESH = pl.DeviceIdType.MESH

F32 = jnp.float32
BF16 = jnp.bfloat16

OFFSETS = sorted(
    [(dx, dy) for dx in range(CTX_X) for dy in range(CTX_Y) if (dx, dy) != (0, 0)],
    key=lambda o: -(min(o[0], CTX_X - o[0]) + min(o[1], CTX_Y - o[1])),
)
TP_OFFSETS = (4, 3, 5, 2, 6, 1, 7)

NN = (((1,), (0,)), ((), ()))
NT = (((1,), (1,)), ((), ()))
TN = (((0,), (0,)), ((), ()))


def dot(a, b, dims):
    return lax.dot_general(a, b, dims, preferred_element_type=F32)


def kernel(
    slopes_in, q_in, k_in, v_in, g_in, c_in, gain_in,
    dq, dk, dv, dg, gain_out,
    slopes, gain_ref, q, k, v, g, c,
    after, before, masked, w_near, w_far, att_t, sca_t, nrm, omg, qs, q_t, ga_t, ga, mem, gm, dki, dvi,
    sums, stats, rcol,
    u, r1, s2, r2, zsend, zrecv, gsend, gpart, gsum, grecv,
    small_sem, load_sem, send1, recv1, send2, recv2, zs_sem, zr_sem, g_sem,
):
    me = lax.axis_index("ctx")
    me_x, me_y = lax.rem(me, CTX_X), lax.div(me, CTX_X)
    my_tp = lax.axis_index("tp")
    my_dp = lax.axis_index("dp")
    ctx_peers = [
        lax.rem(me_y + dy, CTX_Y) * CTX_X + lax.rem(me_x + dx, CTX_X) for dx, dy in OFFSETS
    ]
    tp_peers = [lax.rem(my_tp + o, TP) for o in TP_OFFSETS]
    partner = 1 - my_dp

    def load(n, src, dst, h):
        return pltpu.make_async_copy(
            src.at[0, :, pl.ds(pl.multiple_of(h * HD, HD), HD)], dst.at[h], load_sem.at[n, h]
        )

    def load_kv(h, _):
        load(1, k_in, k, h).start()
        load(2, v_in, v, h).start()
        return 0

    def load_rest(h, _):
        load(0, q_in, q, h).start()
        load(3, g_in, g, h).start()
        load(4, c_in, c, h).start()
        return 0

    def lanes(h):
        return pl.ds(pl.multiple_of(h * HD, HD), HD)

    barrier = pltpu.get_barrier_semaphore()
    for p in ctx_peers:
        pl.semaphore_signal(barrier, inc=1, device_id={"ctx": p}, device_id_type=MESH)
    for p in tp_peers:
        pl.semaphore_signal(barrier, inc=1, device_id={"tp": p}, device_id_type=MESH)
    pl.semaphore_signal(barrier, inc=1, device_id={"dp": partner}, device_id_type=MESH)
    slopes_copy = pltpu.make_async_copy(slopes_in, slopes, small_sem.at[0])
    gain_copy_in = pltpu.make_async_copy(gain_in, gain_ref, small_sem.at[1])
    slopes_copy.start()
    lax.fori_loop(0, PER, load_kv, 0)
    lax.fori_loop(PER, HEADS_HERE, load_kv, 0)
    gain_copy_in.start()
    lax.fori_loop(0, HEADS_HERE, load_rest, 0)
    slopes_copy.wait()

    position = lax.broadcasted_iota(jnp.int32, (BLOCK, HD), 0).astype(F32)
    along = lax.broadcasted_iota(jnp.int32, (1, BLOCK), 1).astype(F32)

    def exchange(src, dst, send, recv, n, p):
        return pltpu.make_async_remote_copy(
            src_ref=src.at[n, p],
            dst_ref=dst.at[n, me],
            send_sem=send.at[n],
            recv_sem=recv.at[n],
            device_id={"ctx": p},
            device_id_type=MESH,
        )

    def send_all(src, dst, send, recv, n):
        for p in ctx_peers:
            exchange(src, dst, send, recv, n, p).start()
        dst[n, me] = src[n, me]

    def waiter(src, dst, send, recv, n):
        return pltpu.make_async_remote_copy(
            src_ref=src.at[n, pl.ds(0, CTX - 1)],
            dst_ref=dst.at[n, pl.ds(0, CTX - 1)],
            send_sem=send.at[n],
            recv_sem=recv.at[n],
            device_id={"ctx": ctx_peers[0]},
            device_id_type=MESH,
        )

    def scan(d, n, reverse):
        waiter(u.at[d], r1.at[d], send1.at[d], recv1.at[d], n).wait_recv()
        fade = jnp.concatenate(
            [
                jnp.exp(jnp.full((PART, HD), -slopes[n * PER + i] * BLOCK, F32))
                for i in range(PER)
            ],
            axis=0,
        )
        total = jnp.zeros((ROWS, HD), F32)
        for b in reversed(range(CTX)) if reverse else range(CTX):
            s2[d, n, b] = total
            total = fade * total + r1[d, n, b]
        send_all(s2.at[d], r2.at[d], send2.at[d], recv2.at[d], n)

    def state(d, n, i):
        return r2[d, n, :, i * PART : (i + 1) * PART, :].reshape(HD, HD).astype(BF16)

    def put(d, n, i, value):
        u[d, n, :, i * PART : (i + 1) * PART, :] = value.reshape(CTX, PART, HD)

    def summary(n):
        for i in range(PER):
            h = n * PER + i
            before[h] = jnp.exp(-slopes[h] * (BLOCK - 1.0 - position))
        for i in range(PER):
            h = n * PER + i
            load(1, k_in, k, h).wait()
            load(2, v_in, v, h).wait()
            scaled_keys = (k[h].astype(F32) * before[h]).astype(BF16)
            put(0, n, i, dot(v[h], scaled_keys, TN))

    def first(n, _):
        summary(n)
        send_all(u.at[0], r1.at[0], send1.at[0], recv1.at[0], n)
        return 0

    summary(0)
    pl.semaphore_wait(barrier, CTX - 1 + TP - 1 + 1)
    send_all(u.at[0], r1.at[0], send1.at[0], recv1.at[0], 0)
    lax.fori_loop(1, CHUNKS, first, 0)

    distance = (
        lax.broadcasted_iota(jnp.int32, (HALF, HALF), 0)
        - lax.broadcasted_iota(jnp.int32, (HALF, HALF), 1)
    ).astype(F32)

    def inside(h, _):
        load(0, q_in, q, h).wait()
        load(3, g_in, g, h).wait()
        load(4, c_in, c, h).wait()
        rate = slopes[h]
        near = jnp.where(distance >= 0.0, jnp.exp(-rate * jnp.maximum(distance, 0.0)), 0.0)
        far = jnp.exp(-rate * (distance + HALF))
        w_near[h] = near
        w_far[h] = far
        top, bottom = q[h, :HALF], q[h, HALF:]
        k_top, k_bottom = k[h, :HALF], k[h, HALF:]
        masked[h, 0] = (dot(top, k_top, NT) * near).astype(BF16)
        masked[h, 1] = (dot(bottom, k_top, NT) * far).astype(BF16)
        masked[h, 2] = (dot(bottom, k_bottom, NT) * near).astype(BF16)
        att_t[h, :, :HALF] = dot(masked[h, 0], v[h, :HALF], NN).T
        att_t[h, :, HALF:] = (
            dot(masked[h, 1], v[h, :HALF], NN) + dot(masked[h, 2], v[h, HALF:], NN)
        ).T
        weight = jnp.exp(-rate * (position + 1.0))
        after[h] = weight
        qs[h] = (q[h].astype(F32) * weight).astype(BF16)
        q_t[h] = q[h].T
        gated = 1.0 / (1.0 + jnp.exp(-g[h].astype(F32)))
        normed = c[h].astype(F32) * gated
        nrm[h] = normed
        sca_t[h] = (normed * gain_ref[pl.ds(h, 1), :]).T
        omg[h] = 1.0 - gated
        return 0

    def scan_forward(n, _):
        scan(0, n, False)
        return 0

    gain_copy_in.wait()
    lax.fori_loop(0, HEADS_HERE // 2, inside, 0)
    lax.fori_loop(0, CHUNKS, scan_forward, 0)
    lax.fori_loop(HEADS_HERE // 2, HEADS_HERE, inside, 0)

    sums[...] = jnp.zeros_like(sums)

    def attend(n, _):
        waiter(s2.at[0], r2.at[0], send2.at[0], recv2.at[0], n).wait_recv()
        for i in range(PER):
            h = n * PER + i
            memory = state(0, n, i)
            mem[h] = memory
            fade = jnp.exp(-slopes[h] * (along + 1.0))
            attended = att_t[h] + fade * dot(memory, q_t[h], NN)
            att_t[h] = attended
            sums[0] += jnp.sum((attended * attended).reshape(HD // 8, 8, BLOCK), axis=0)
            sums[1] += jnp.sum((sca_t[h] * attended).reshape(HD // 8, 8, BLOCK), axis=0)
        return 0

    lax.fori_loop(0, CHUNKS, attend, 0)
    rows = []
    for n in range(2):
        row = jnp.sum(sums[n], axis=0, keepdims=True)
        rows += [row[:, t * HD : (t + 1) * HD] for t in range(BLOCK // HD)]
    zsend[...] = jnp.concatenate(rows, axis=0)

    def tp_copy(i):
        return pltpu.make_async_remote_copy(
            src_ref=zsend,
            dst_ref=zrecv.at[my_tp],
            send_sem=zs_sem.at[i],
            recv_sem=zr_sem.at[i],
            device_id={"tp": tp_peers[i]},
            device_id_type=MESH,
        )

    for i in range(TP - 1):
        tp_copy(i).start()
    zrecv[my_tp] = zsend[...]
    for i in range(TP - 1):
        tp_copy(i).wait_recv()
    totals = zrecv[0]
    for i in range(1, TP):
        totals = totals + zrecv[i]
    radius = lax.rsqrt(totals[:4] / FEATURES + EPSILON)
    cross = radius * radius * radius * totals[4:] / FEATURES
    stats[0] = jnp.concatenate([radius[t : t + 1] for t in range(4)], axis=1)
    stats[1] = jnp.concatenate([cross[t : t + 1] for t in range(4)], axis=1)

    def second(n, _):
        for i in range(PER):
            h = n * PER + i
            gradient = (stats[0] * sca_t[h] - stats[1] * att_t[h]).astype(BF16)
            ga_t[h] = gradient
            put(1, n, i, dot(gradient, qs[h], NN))
        send_all(u.at[1], r1.at[1], send1.at[1], recv1.at[1], n)
        return 0

    lax.fori_loop(0, CHUNKS, second, 0)

    for t in range(BLOCK // HD):
        column = stats[0, :, t * HD : (t + 1) * HD]
        rcol[t * HD : (t + 1) * HD, :] = jnp.broadcast_to(column, (HD, HD)).T

    def gate(h, _):
        ga[h] = ga_t[h].T
        common = nrm[h] * att_t[h].T * rcol[...]
        gsend[pl.ds(h, 1), :] = jnp.sum(common, axis=0, keepdims=True)
        dg[:, lanes(h)] = (common * gain_ref[pl.ds(h, 1), :] * omg[h]).astype(BF16)
        return 0

    lax.fori_loop(0, HEADS_HERE, gate, 0)
    pair = pltpu.make_async_remote_copy(
        src_ref=gsend,
        dst_ref=gpart,
        send_sem=g_sem.at[0],
        recv_sem=g_sem.at[1],
        device_id={"dp": partner},
        device_id_type=MESH,
    )
    pair.start()

    def backward(h, _):
        gradient = ga[h]
        g_top, g_bottom = ga[h, :HALF], ga[h, HALF:]
        v_top, v_bottom = v[h, :HALF], v[h, HALF:]
        near, far = w_near[h], w_far[h]
        m0 = (dot(g_top, v_top, NT) * near).astype(BF16)
        m1 = (dot(g_bottom, v_top, NT) * far).astype(BF16)
        m2 = (dot(g_bottom, v_bottom, NT) * near).astype(BF16)
        gm[0] = m0
        gm[1] = m1
        gm[2] = m2
        k_top, k_bottom = k[h, :HALF], k[h, HALF:]
        carried = after[h] * dot(gradient, mem[h], NN)
        dq[:HALF, lanes(h)] = (dot(gm[0], k_top, NN) + carried[:HALF]).astype(BF16)
        dq[HALF:, lanes(h)] = (
            dot(gm[1], k_top, NN) + dot(gm[2], k_bottom, NN) + carried[HALF:]
        ).astype(BF16)
        dki[h, :HALF] = dot(gm[0], q[h, :HALF], TN) + dot(gm[1], q[h, HALF:], TN)
        dki[h, HALF:] = dot(gm[2], q[h, HALF:], TN)
        dvi[h, :HALF] = dot(masked[h, 0], g_top, TN) + dot(masked[h, 1], g_bottom, TN)
        dvi[h, HALF:] = dot(masked[h, 2], g_bottom, TN)
        return 0

    def scan_backward(n, _):
        scan(1, n, True)
        return 0

    lax.fori_loop(0, 3, backward, 0)
    pair.wait_recv()
    gsum[0] = gsend[...] + gpart[...]

    def gain_copy(stage, o):
        place = lax.rem((me_x, me_y)[stage] + o, 4)
        return pltpu.make_async_remote_copy(
            src_ref=gsum.at[stage],
            dst_ref=grecv.at[stage, (me_x, me_y)[stage]],
            send_sem=g_sem.at[2 + 2 * stage],
            recv_sem=g_sem.at[3 + 2 * stage],
            device_id={"ctx": (me_y * CTX_X + place, place * CTX_X + me_x)[stage]},
            device_id_type=MESH,
        )

    def gain_start(stage):
        for o in (2, 1, 3):
            gain_copy(stage, o).start()
        grecv[stage, (me_x, me_y)[stage]] = gsum[stage]

    def gain_all(stage):
        return pltpu.make_async_remote_copy(
            src_ref=grecv.at[stage, pl.ds(0, 3)],
            dst_ref=grecv.at[stage, pl.ds(0, 3)],
            send_sem=g_sem.at[2 + 2 * stage],
            recv_sem=g_sem.at[3 + 2 * stage],
            device_id={"ctx": ctx_peers[0]},
            device_id_type=MESH,
        )

    gain_start(0)
    lax.fori_loop(0, CHUNKS, scan_backward, 0)
    gain_all(0).wait_recv()
    gsum[1] = grecv[0, 0] + grecv[0, 1] + grecv[0, 2] + grecv[0, 3]
    gain_start(1)
    lax.fori_loop(3, HEADS_HERE, backward, 0)

    def sent(n, _):
        waiter(u.at[0], r1.at[0], send1.at[0], recv1.at[0], n).wait_send()
        waiter(s2.at[0], r2.at[0], send2.at[0], recv2.at[0], n).wait_send()
        waiter(u.at[1], r1.at[1], send1.at[1], recv1.at[1], n).wait_send()
        return 0

    lax.fori_loop(0, CHUNKS, sent, 0)
    for i in range(TP - 1):
        tp_copy(i).wait_send()
    pair.wait_send()

    def finish(n, _):
        waiter(s2.at[1], r2.at[1], send2.at[1], recv2.at[1], n).wait_recv()
        for i in range(PER):
            h = n * PER + i
            recalled = state(1, n, i)
            dk[:, lanes(h)] = (dki[h] + before[h] * dot(v[h], recalled, NN)).astype(BF16)
            dv[:, lanes(h)] = (dvi[h] + before[h] * dot(k[h], recalled, NT)).astype(BF16)
        return 0

    lax.fori_loop(0, CHUNKS, finish, 0)

    gain_all(1).wait_recv()
    gain_out[...] = grecv[1, 0] + grecv[1, 1] + grecv[1, 2] + grecv[1, 3]
    gain_all(0).wait_send()
    gain_all(1).wait_send()

    def drain(n, _):
        waiter(s2.at[1], r2.at[1], send2.at[1], recv2.at[1], n).wait_send()
        return 0

    lax.fori_loop(0, CHUNKS, drain, 0)


def place(dq_in, dk_in, dv_in, dg_in, gain_in, dq, dk, dv, dg, gain, sem):
    pairs = ((dq_in, dq), (dk_in, dk), (dv_in, dv), (dg_in, dg))
    copies = [
        pltpu.make_async_copy(
            src.at[pl.ds(i * PIECE, PIECE)], dst.at[0, pl.ds(i * PIECE, PIECE)], sem.at[n, i]
        )
        for i in range(BLOCK // PIECE)
        for n, (src, dst) in enumerate(pairs)
    ]
    for copy in copies:
        copy.start()
    gain[...] = gain_in[...]
    for copy in copies:
        copy.wait()


def per_device(queries, keys, values, gate, cotangent, gain, slopes):
    whole = jax.ShapeDtypeStruct((1, BLOCK, HEADS_HERE * HD), BF16)
    flat = pltpu.VMEM((BLOCK, HEADS_HERE * HD), BF16)
    heads16 = pltpu.VMEM((HEADS_HERE, BLOCK, HD), BF16)
    heads32 = pltpu.VMEM((HEADS_HERE, BLOCK, HD), F32)
    heads16_t = pltpu.VMEM((HEADS_HERE, HD, BLOCK), BF16)
    heads32_t = pltpu.VMEM((HEADS_HERE, HD, BLOCK), F32)
    travel = pltpu.VMEM((2, CHUNKS, CTX, ROWS, HD), F32)
    tile = pltpu.VMEM((HEADS_HERE, HD), F32)
    dma = pltpu.SemaphoreType.DMA
    scratch = (
        [pltpu.SMEM((HEADS_HERE,), F32), tile]
        + [heads16] * 5
        + [
            heads32,
            heads32,
            pltpu.VMEM((HEADS_HERE, 3, HALF, HALF), BF16),
            pltpu.VMEM((HEADS_HERE, HALF, HALF), F32),
            pltpu.VMEM((HEADS_HERE, HALF, HALF), F32),
            heads32_t,
            heads32_t,
            heads32,
            heads32,
            heads16,
            heads16_t,
            heads16_t,
            heads16,
            pltpu.VMEM((HEADS_HERE, HD, HD), BF16),
            pltpu.VMEM((3, HALF, HALF), BF16),
            heads32,
            heads32,
        ]
        + [
            pltpu.VMEM((2, 8, BLOCK), F32),
            pltpu.VMEM((2, 1, BLOCK), F32),
            pltpu.VMEM((BLOCK, HD), F32),
        ]
        + [travel] * 4
        + [
            tile,
            pltpu.VMEM((TP, 8, HD), F32),
            tile,
            tile,
            pltpu.VMEM((2, HEADS_HERE, HD), F32),
            pltpu.VMEM((2, 4, HEADS_HERE, HD), F32),
            dma((2,)),
            dma((5, HEADS_HERE)),
        ]
        + [dma((2, CHUNKS))] * 4
        + [dma((TP - 1,)), dma((TP - 1,)), dma((6,))]
    )
    anywhere = pl.BlockSpec(memory_space=pl.ANY)
    in_hbm = pl.BlockSpec(memory_space=pltpu.HBM)
    in_vmem = pl.BlockSpec(memory_space=pltpu.VMEM)
    flops = HEADS_HERE * BLOCK * HD * 2 * (6 * BLOCK * 3 // 4 + 6 * HD)
    whole_inputs = [
        pltpu.with_memory_space_constraint(x, pltpu.HBM)
        for x in (
            slopes, queries, keys, values, gate, cotangent, gain.reshape(HEADS_HERE, HD)
        )
    ]
    results = pl.pallas_call(
        kernel,
        out_shape=(flat, flat, flat, flat, tile),
        in_specs=[in_hbm] * 7,
        out_specs=(in_vmem,) * 5,
        scratch_shapes=scratch,
        compiler_params=pltpu.CompilerParams(
            collective_id=0, has_side_effects=True, vmem_limit_bytes=44 << 20
        ),
        cost_estimate=pl.CostEstimate(
            flops=flops, bytes_accessed=5 << 20, transcendentals=HEADS_HERE * BLOCK * BLOCK
        ),
        name="lightning_backward",
    )(*whole_inputs)
    results = [pltpu.with_memory_space_constraint(x, pltpu.VMEM) for x in results]
    dq, dk, dv, dg, total = pl.pallas_call(
        place,
        out_shape=(whole, whole, whole, whole, jax.ShapeDtypeStruct((HEADS_HERE, HD), F32)),
        in_specs=[in_vmem] * 5,
        out_specs=(anywhere,) * 4 + (in_vmem,),
        scratch_shapes=[dma((4, BLOCK // PIECE))],
        compiler_params=pltpu.CompilerParams(vmem_limit_bytes=2 << 20),
        cost_estimate=pl.CostEstimate(flops=0, bytes_accessed=8 << 20, transcendentals=0),
        name="place_results",
    )(*results)
    return dq, dk, dv, dg, total.reshape(HEADS_HERE * HD)


def solution(mesh):
    wide = P("dp", "ctx", "tp")
    return jax.shard_map(
        per_device,
        mesh=mesh,
        in_specs=(wide, wide, wide, wide, wide, P("tp"), P("tp")),
        out_specs=(wide, wide, wide, wide, P("tp")),
        check_vma=False,
    )
```

```python
import functools

import jax
import jax.numpy as jnp
from jax import lax
from jax.experimental import pallas as pl
from jax.experimental.pallas import tpu as pltpu
from jax.sharding import PartitionSpec as P

HD = 128
BLOCK = 512
FEATURES = 8192
HEADS_HERE = 8
HALF = BLOCK // 2
CTX_X = 4
CTX_Y = 4
CTX = CTX_X * CTX_Y
TP = 8
CHUNKS = 4
PER = HEADS_HERE // CHUNKS
PART = HD // CTX
PIECE = 512
ROWS = PER * PART
EPSILON = 1e-05
MESH = pl.DeviceIdType.MESH

F32 = jnp.float32
BF16 = jnp.bfloat16

OFFSETS = sorted(
    [(dx, dy) for dx in range(CTX_X) for dy in range(CTX_Y) if (dx, dy) != (0, 0)],
    key=lambda o: -(min(o[0], CTX_X - o[0]) + min(o[1], CTX_Y - o[1])),
)
TP_OFFSETS = (4, 3, 5, 2, 6, 1, 7)

NN = (((1,), (0,)), ((), ()))
NT = (((1,), (1,)), ((), ()))
TN = (((0,), (0,)), ((), ()))


def dot(a, b, dims):
    return lax.dot_general(a, b, dims, preferred_element_type=F32)


def kernel(
    slopes_in, q_in, k_in, v_in, g_in, c_in, gain_in,
    dq, dk, dv, dg, gain_out,
    slopes, gain_ref, q, k, v, g, c,
    after, before, masked, w_near, w_far, att_t, sca_t, nrm, omg, qs, q_t, ga_t, ga, mem, gm, dki, dvi,
    sums, stats, rcol,
    u, r1, s2, r2, zsend, zrecv, gsend, gpart, gsum, grecv,
    small_sem, load_sem, send1, recv1, send2, recv2, zs_sem, zr_sem, g_sem,
):
    me = lax.axis_index("ctx")
    me_x, me_y = lax.rem(me, CTX_X), lax.div(me, CTX_X)
    my_tp = lax.axis_index("tp")
    my_dp = lax.axis_index("dp")
    ctx_peers = [
        lax.rem(me_y + dy, CTX_Y) * CTX_X + lax.rem(me_x + dx, CTX_X) for dx, dy in OFFSETS
    ]
    tp_peers = [lax.rem(my_tp + o, TP) for o in TP_OFFSETS]
    partner = 1 - my_dp

    def load(n, src, dst, h):
        return pltpu.make_async_copy(
            src.at[0, :, pl.ds(pl.multiple_of(h * HD, HD), HD)], dst.at[h], load_sem.at[n, h]
        )

    def load_kv(h, _):
        load(1, k_in, k, h).start()
        load(2, v_in, v, h).start()
        return 0

    def load_rest(h, _):
        load(0, q_in, q, h).start()
        load(3, g_in, g, h).start()
        load(4, c_in, c, h).start()
        return 0

    def lanes(h):
        return pl.ds(pl.multiple_of(h * HD, HD), HD)

    barrier = pltpu.get_barrier_semaphore()
    for p in ctx_peers:
        pl.semaphore_signal(barrier, inc=1, device_id={"ctx": p}, device_id_type=MESH)
    for p in tp_peers:
        pl.semaphore_signal(barrier, inc=1, device_id={"tp": p}, device_id_type=MESH)
    pl.semaphore_signal(barrier, inc=1, device_id={"dp": partner}, device_id_type=MESH)
    slopes_copy = pltpu.make_async_copy(slopes_in, slopes, small_sem.at[0])
    gain_copy_in = pltpu.make_async_copy(gain_in, gain_ref, small_sem.at[1])
    slopes_copy.start()
    lax.fori_loop(0, PER, load_kv, 0)
    lax.fori_loop(PER, HEADS_HERE, load_kv, 0)
    gain_copy_in.start()
    lax.fori_loop(0, HEADS_HERE, load_rest, 0)
    slopes_copy.wait()

    position = lax.broadcasted_iota(jnp.int32, (BLOCK, HD), 0).astype(F32)
    along = lax.broadcasted_iota(jnp.int32, (1, BLOCK), 1).astype(F32)

    def exchange(src, dst, send, recv, n, p):
        return pltpu.make_async_remote_copy(
            src_ref=src.at[n, p],
            dst_ref=dst.at[n, me],
            send_sem=send.at[n],
            recv_sem=recv.at[n],
            device_id={"ctx": p},
            device_id_type=MESH,
        )

    def send_all(src, dst, send, recv, n):
        for p in ctx_peers:
            exchange(src, dst, send, recv, n, p).start()
        dst[n, me] = src[n, me]

    def waiter(src, dst, send, recv, n):
        return pltpu.make_async_remote_copy(
            src_ref=src.at[n, pl.ds(0, CTX - 1)],
            dst_ref=dst.at[n, pl.ds(0, CTX - 1)],
            send_sem=send.at[n],
            recv_sem=recv.at[n],
            device_id={"ctx": ctx_peers[0]},
            device_id_type=MESH,
        )

    def scan(d, n, reverse):
        waiter(u.at[d], r1.at[d], send1.at[d], recv1.at[d], n).wait_recv()
        fade = jnp.concatenate(
            [
                jnp.exp(jnp.full((PART, HD), -slopes[n * PER + i] * BLOCK, F32))
                for i in range(PER)
            ],
            axis=0,
        )
        total = jnp.zeros((ROWS, HD), F32)
        for b in reversed(range(CTX)) if reverse else range(CTX):
            s2[d, n, b] = total
            total = fade * total + r1[d, n, b]
        send_all(s2.at[d], r2.at[d], send2.at[d], recv2.at[d], n)

    def state(d, n, i):
        return r2[d, n, :, i * PART : (i + 1) * PART, :].reshape(HD, HD).astype(BF16)

    def put(d, n, i, value):
        u[d, n, :, i * PART : (i + 1) * PART, :] = value.reshape(CTX, PART, HD)

    def summary(n):
        for i in range(PER):
            h = n * PER + i
            before[h] = jnp.exp(-slopes[h] * (BLOCK - 1.0 - position))
        for i in range(PER):
            h = n * PER + i
            load(1, k_in, k, h).wait()
            load(2, v_in, v, h).wait()
            scaled_keys = (k[h].astype(F32) * before[h]).astype(BF16)
            put(0, n, i, dot(v[h], scaled_keys, TN))

    def first(n, _):
        summary(n)
        send_all(u.at[0], r1.at[0], send1.at[0], recv1.at[0], n)
        return 0

    summary(0)
    pl.semaphore_wait(barrier, CTX - 1 + TP - 1 + 1)
    send_all(u.at[0], r1.at[0], send1.at[0], recv1.at[0], 0)
    lax.fori_loop(1, CHUNKS, first, 0)

    distance = (
        lax.broadcasted_iota(jnp.int32, (HALF, HALF), 0)
        - lax.broadcasted_iota(jnp.int32, (HALF, HALF), 1)
    ).astype(F32)

    def inside(h, _):
        load(0, q_in, q, h).wait()
        load(3, g_in, g, h).wait()
        load(4, c_in, c, h).wait()
        rate = slopes[h]
        near = jnp.where(distance >= 0.0, jnp.exp(-rate * jnp.maximum(distance, 0.0)), 0.0)
        far = jnp.exp(-rate * (distance + HALF))
        w_near[h] = near
        w_far[h] = far
        top, bottom = q[h, :HALF], q[h, HALF:]
        k_top, k_bottom = k[h, :HALF], k[h, HALF:]
        masked[h, 0] = (dot(top, k_top, NT) * near).astype(BF16)
        masked[h, 1] = (dot(bottom, k_top, NT) * far).astype(BF16)
        masked[h, 2] = (dot(bottom, k_bottom, NT) * near).astype(BF16)
        att_t[h, :, :HALF] = dot(masked[h, 0], v[h, :HALF], NN).T
        att_t[h, :, HALF:] = (
            dot(masked[h, 1], v[h, :HALF], NN) + dot(masked[h, 2], v[h, HALF:], NN)
        ).T
        weight = jnp.exp(-rate * (position + 1.0))
        after[h] = weight
        qs[h] = (q[h].astype(F32) * weight).astype(BF16)
        q_t[h] = q[h].T
        gated = 1.0 / (1.0 + jnp.exp(-g[h].astype(F32)))
        normed = c[h].astype(F32) * gated
        nrm[h] = normed
        sca_t[h] = (normed * gain_ref[pl.ds(h, 1), :]).T
        omg[h] = 1.0 - gated
        return 0

    def scan_forward(n, _):
        scan(0, n, False)
        return 0

    gain_copy_in.wait()
    lax.fori_loop(0, HEADS_HERE // 2, inside, 0)
    lax.fori_loop(0, CHUNKS, scan_forward, 0)
    lax.fori_loop(HEADS_HERE // 2, HEADS_HERE, inside, 0)

    sums[...] = jnp.zeros_like(sums)

    def attend(n, _):
        waiter(s2.at[0], r2.at[0], send2.at[0], recv2.at[0], n).wait_recv()
        for i in range(PER):
            h = n * PER + i
            memory = state(0, n, i)
            mem[h] = memory
            fade = jnp.exp(-slopes[h] * (along + 1.0))
            attended = att_t[h] + fade * dot(memory, q_t[h], NN)
            att_t[h] = attended
            sums[0] += jnp.sum((attended * attended).reshape(HD // 8, 8, BLOCK), axis=0)
            sums[1] += jnp.sum((sca_t[h] * attended).reshape(HD // 8, 8, BLOCK), axis=0)
        return 0

    lax.fori_loop(0, CHUNKS, attend, 0)
    rows = []
    for n in range(2):
        row = jnp.sum(sums[n], axis=0, keepdims=True)
        rows += [row[:, t * HD : (t + 1) * HD] for t in range(BLOCK // HD)]
    zsend[...] = jnp.concatenate(rows, axis=0)

    def tp_copy(i):
        return pltpu.make_async_remote_copy(
            src_ref=zsend,
            dst_ref=zrecv.at[my_tp],
            send_sem=zs_sem.at[i],
            recv_sem=zr_sem.at[i],
            device_id={"tp": tp_peers[i]},
            device_id_type=MESH,
        )

    for i in range(TP - 1):
        tp_copy(i).start()
    zrecv[my_tp] = zsend[...]
    for i in range(TP - 1):
        tp_copy(i).wait_recv()
    totals = zrecv[0]
    for i in range(1, TP):
        totals = totals + zrecv[i]
    radius = lax.rsqrt(totals[:4] / FEATURES + EPSILON)
    cross = radius * radius * radius * totals[4:] / FEATURES
    stats[0] = jnp.concatenate([radius[t : t + 1] for t in range(4)], axis=1)
    stats[1] = jnp.concatenate([cross[t : t + 1] for t in range(4)], axis=1)

    def second(n, _):
        for i in range(PER):
            h = n * PER + i
            gradient = (stats[0] * sca_t[h] - stats[1] * att_t[h]).astype(BF16)
            ga_t[h] = gradient
            put(1, n, i, dot(gradient, qs[h], NN))
        send_all(u.at[1], r1.at[1], send1.at[1], recv1.at[1], n)
        return 0

    lax.fori_loop(0, CHUNKS, second, 0)

    for t in range(BLOCK // HD):
        column = stats[0, :, t * HD : (t + 1) * HD]
        rcol[t * HD : (t + 1) * HD, :] = jnp.broadcast_to(column, (HD, HD)).T

    def gate(h, _):
        ga[h] = ga_t[h].T
        common = nrm[h] * att_t[h].T * rcol[...]
        gsend[pl.ds(h, 1), :] = jnp.sum(common, axis=0, keepdims=True)
        dg[:, lanes(h)] = (common * gain_ref[pl.ds(h, 1), :] * omg[h]).astype(BF16)
        return 0

    lax.fori_loop(0, HEADS_HERE, gate, 0)
    pair = pltpu.make_async_remote_copy(
        src_ref=gsend,
        dst_ref=gpart,
        send_sem=g_sem.at[0],
        recv_sem=g_sem.at[1],
        device_id={"dp": partner},
        device_id_type=MESH,
    )
    pair.start()

    def backward(h, _):
        gradient = ga[h]
        g_top, g_bottom = ga[h, :HALF], ga[h, HALF:]
        v_top, v_bottom = v[h, :HALF], v[h, HALF:]
        near, far = w_near[h], w_far[h]
        m0 = (dot(g_top, v_top, NT) * near).astype(BF16)
        m1 = (dot(g_bottom, v_top, NT) * far).astype(BF16)
        m2 = (dot(g_bottom, v_bottom, NT) * near).astype(BF16)
        gm[0] = m0
        gm[1] = m1
        gm[2] = m2
        k_top, k_bottom = k[h, :HALF], k[h, HALF:]
        carried = after[h] * dot(gradient, mem[h], NN)
        dq[:HALF, lanes(h)] = (dot(gm[0], k_top, NN) + carried[:HALF]).astype(BF16)
        dq[HALF:, lanes(h)] = (
            dot(gm[1], k_top, NN) + dot(gm[2], k_bottom, NN) + carried[HALF:]
        ).astype(BF16)
        dki[h, :HALF] = dot(gm[0], q[h, :HALF], TN) + dot(gm[1], q[h, HALF:], TN)
        dki[h, HALF:] = dot(gm[2], q[h, HALF:], TN)
        dvi[h, :HALF] = dot(masked[h, 0], g_top, TN) + dot(masked[h, 1], g_bottom, TN)
        dvi[h, HALF:] = dot(masked[h, 2], g_bottom, TN)
        return 0

    def scan_backward(n, _):
        scan(1, n, True)
        return 0

    lax.fori_loop(0, 3, backward, 0)
    pair.wait_recv()
    gsum[0] = gsend[...] + gpart[...]

    def gain_copy(stage, o):
        place = lax.rem((me_x, me_y)[stage] + o, 4)
        return pltpu.make_async_remote_copy(
            src_ref=gsum.at[stage],
            dst_ref=grecv.at[stage, (me_x, me_y)[stage]],
            send_sem=g_sem.at[2 + 2 * stage],
            recv_sem=g_sem.at[3 + 2 * stage],
            device_id={"ctx": (me_y * CTX_X + place, place * CTX_X + me_x)[stage]},
            device_id_type=MESH,
        )

    def gain_start(stage):
        for o in (2, 1, 3):
            gain_copy(stage, o).start()
        grecv[stage, (me_x, me_y)[stage]] = gsum[stage]

    def gain_all(stage):
        return pltpu.make_async_remote_copy(
            src_ref=grecv.at[stage, pl.ds(0, 3)],
            dst_ref=grecv.at[stage, pl.ds(0, 3)],
            send_sem=g_sem.at[2 + 2 * stage],
            recv_sem=g_sem.at[3 + 2 * stage],
            device_id={"ctx": ctx_peers[0]},
            device_id_type=MESH,
        )

    gain_start(0)
    lax.fori_loop(0, CHUNKS, scan_backward, 0)
    gain_all(0).wait_recv()
    gsum[1] = grecv[0, 0] + grecv[0, 1] + grecv[0, 2] + grecv[0, 3]
    gain_start(1)
    lax.fori_loop(3, HEADS_HERE, backward, 0)

    def sent(n, _):
        waiter(u.at[0], r1.at[0], send1.at[0], recv1.at[0], n).wait_send()
        waiter(s2.at[0], r2.at[0], send2.at[0], recv2.at[0], n).wait_send()
        waiter(u.at[1], r1.at[1], send1.at[1], recv1.at[1], n).wait_send()
        return 0

    lax.fori_loop(0, CHUNKS, sent, 0)
    for i in range(TP - 1):
        tp_copy(i).wait_send()
    pair.wait_send()

    def finish(n, _):
        waiter(s2.at[1], r2.at[1], send2.at[1], recv2.at[1], n).wait_recv()
        for i in range(PER):
            h = n * PER + i
            recalled = state(1, n, i)
            dk[:, lanes(h)] = (dki[h] + before[h] * dot(v[h], recalled, NN)).astype(BF16)
            dv[:, lanes(h)] = (dvi[h] + before[h] * dot(k[h], recalled, NT)).astype(BF16)
        return 0

    lax.fori_loop(0, CHUNKS, finish, 0)

    gain_all(1).wait_recv()
    gain_out[...] = grecv[1, 0] + grecv[1, 1] + grecv[1, 2] + grecv[1, 3]
    gain_all(0).wait_send()
    gain_all(1).wait_send()

    def drain(n, _):
        waiter(s2.at[1], r2.at[1], send2.at[1], recv2.at[1], n).wait_send()
        return 0

    lax.fori_loop(0, CHUNKS, drain, 0)


def place(dq_in, dk_in, dv_in, dg_in, gain_in, dq, dk, dv, dg, gain, sem, gain_sem):
    pairs = ((dq_in, dq), (dk_in, dk), (dv_in, dv), (dg_in, dg))
    copies = [
        pltpu.make_async_copy(
            src.at[pl.ds(i * PIECE, PIECE)], dst.at[0, pl.ds(i * PIECE, PIECE)], sem.at[n, i]
        )
        for i in range(BLOCK // PIECE)
        for n, (src, dst) in enumerate(pairs)
    ]
    copies.append(pltpu.make_async_copy(gain_in, gain, gain_sem))
    for copy in copies:
        copy.start()
    for copy in copies:
        copy.wait()


def per_device(queries, keys, values, gate, cotangent, gain, slopes):
    whole = jax.ShapeDtypeStruct((1, BLOCK, HEADS_HERE * HD), BF16)
    flat = pltpu.VMEM((BLOCK, HEADS_HERE * HD), BF16)
    heads16 = pltpu.VMEM((HEADS_HERE, BLOCK, HD), BF16)
    heads32 = pltpu.VMEM((HEADS_HERE, BLOCK, HD), F32)
    heads16_t = pltpu.VMEM((HEADS_HERE, HD, BLOCK), BF16)
    heads32_t = pltpu.VMEM((HEADS_HERE, HD, BLOCK), F32)
    travel = pltpu.VMEM((2, CHUNKS, CTX, ROWS, HD), F32)
    tile = pltpu.VMEM((HEADS_HERE, HD), F32)
    dma = pltpu.SemaphoreType.DMA
    scratch = (
        [pltpu.SMEM((HEADS_HERE,), F32), tile]
        + [heads16] * 5
        + [
            heads32,
            heads32,
            pltpu.VMEM((HEADS_HERE, 3, HALF, HALF), BF16),
            pltpu.VMEM((HEADS_HERE, HALF, HALF), F32),
            pltpu.VMEM((HEADS_HERE, HALF, HALF), F32),
            heads32_t,
            heads32_t,
            heads32,
            heads32,
            heads16,
            heads16_t,
            heads16_t,
            heads16,
            pltpu.VMEM((HEADS_HERE, HD, HD), BF16),
            pltpu.VMEM((3, HALF, HALF), BF16),
            heads32,
            heads32,
        ]
        + [
            pltpu.VMEM((2, 8, BLOCK), F32),
            pltpu.VMEM((2, 1, BLOCK), F32),
            pltpu.VMEM((BLOCK, HD), F32),
        ]
        + [travel] * 4
        + [
            tile,
            pltpu.VMEM((TP, 8, HD), F32),
            tile,
            tile,
            pltpu.VMEM((2, HEADS_HERE, HD), F32),
            pltpu.VMEM((2, 4, HEADS_HERE, HD), F32),
            dma((2,)),
            dma((5, HEADS_HERE)),
        ]
        + [dma((2, CHUNKS))] * 4
        + [dma((TP - 1,)), dma((TP - 1,)), dma((6,))]
    )
    anywhere = pl.BlockSpec(memory_space=pl.ANY)
    in_hbm = pl.BlockSpec(memory_space=pltpu.HBM)
    in_vmem = pl.BlockSpec(memory_space=pltpu.VMEM)
    flops = HEADS_HERE * BLOCK * HD * 2 * (6 * BLOCK * 3 // 4 + 6 * HD)
    whole_inputs = [
        pltpu.with_memory_space_constraint(x, pltpu.HBM)
        for x in (
            slopes, queries, keys, values, gate, cotangent, gain.reshape(HEADS_HERE, HD)
        )
    ]
    results = pl.pallas_call(
        kernel,
        out_shape=(flat, flat, flat, flat, tile),
        in_specs=[in_hbm] * 7,
        out_specs=(in_vmem,) * 5,
        scratch_shapes=scratch,
        compiler_params=pltpu.CompilerParams(
            collective_id=0, has_side_effects=True, vmem_limit_bytes=44 << 20
        ),
        cost_estimate=pl.CostEstimate(
            flops=flops, bytes_accessed=5 << 20, transcendentals=HEADS_HERE * BLOCK * BLOCK
        ),
        name="lightning_backward",
    )(*whole_inputs)
    results = [pltpu.with_memory_space_constraint(x, pltpu.VMEM) for x in results]
    dq, dk, dv, dg, total = pl.pallas_call(
        place,
        out_shape=(whole, whole, whole, whole, jax.ShapeDtypeStruct((HEADS_HERE, HD), F32)),
        in_specs=[in_vmem] * 5,
        out_specs=(anywhere,) * 5,
        scratch_shapes=[dma((4, BLOCK // PIECE)), dma],
        compiler_params=pltpu.CompilerParams(vmem_limit_bytes=2 << 20),
        cost_estimate=pl.CostEstimate(flops=0, bytes_accessed=8 << 20, transcendentals=0),
        name="place_results",
    )(*results)
    return dq, dk, dv, dg, total.reshape(HEADS_HERE * HD)


def solution(mesh):
    wide = P("dp", "ctx", "tp")
    return jax.shard_map(
        per_device,
        mesh=mesh,
        in_specs=(wide, wide, wide, wide, wide, P("tp"), P("tp")),
        out_specs=(wide, wide, wide, wide, P("tp")),
        check_vma=False,
    )
```

```python
import functools

import jax
import jax.numpy as jnp
from jax import lax
from jax.experimental import pallas as pl
from jax.experimental.pallas import tpu as pltpu
from jax.sharding import PartitionSpec as P

HD = 128
BLOCK = 512
FEATURES = 8192
HEADS_HERE = 8
HALF = BLOCK // 2
CTX_X = 4
CTX_Y = 4
CTX = CTX_X * CTX_Y
TP = 8
CHUNKS = 4
PER = HEADS_HERE // CHUNKS
PART = HD // CTX
PIECE = 512
ROWS = PER * PART
EPSILON = 1e-05
MESH = pl.DeviceIdType.MESH

F32 = jnp.float32
BF16 = jnp.bfloat16

OFFSETS = sorted(
    [(dx, dy) for dx in range(CTX_X) for dy in range(CTX_Y) if (dx, dy) != (0, 0)],
    key=lambda o: -(min(o[0], CTX_X - o[0]) + min(o[1], CTX_Y - o[1])),
)
TP_OFFSETS = (4, 3, 5, 2, 6, 1, 7)

NN = (((1,), (0,)), ((), ()))
NT = (((1,), (1,)), ((), ()))
TN = (((0,), (0,)), ((), ()))


def dot(a, b, dims):
    return lax.dot_general(a, b, dims, preferred_element_type=F32)


def kernel(
    slopes_in, q_in, k_in, v_in, g_in, c_in, gain_in,
    dq, dk, dv, dg, gain_out,
    slopes, gain_ref, q, k, v, g, c,
    after, before, masked, w_near, w_far, att_t, sca_t, nrm, omg, qs, q_t, ga_t, ga, mem, gm, dki, dvi,
    sums, stats, rcol,
    u, r1, s2, r2, zsend, zrecv, gsend, gpart, gsum, grecv,
    small_sem, load_sem, send1, recv1, send2, recv2, zs_sem, zr_sem, g_sem,
):
    me = lax.axis_index("ctx")
    me_x, me_y = lax.rem(me, CTX_X), lax.div(me, CTX_X)
    my_tp = lax.axis_index("tp")
    my_dp = lax.axis_index("dp")
    ctx_peers = [
        lax.rem(me_y + dy, CTX_Y) * CTX_X + lax.rem(me_x + dx, CTX_X) for dx, dy in OFFSETS
    ]
    tp_peers = [lax.rem(my_tp + o, TP) for o in TP_OFFSETS]
    partner = 1 - my_dp

    def load(n, src, dst, h):
        return pltpu.make_async_copy(
            src.at[0, :, pl.ds(pl.multiple_of(h * HD, HD), HD)], dst.at[h], load_sem.at[n, h]
        )

    def load_kv(h, _):
        load(1, k_in, k, h).start()
        load(2, v_in, v, h).start()
        return 0

    def load_rest(h, _):
        load(0, q_in, q, h).start()
        load(3, g_in, g, h).start()
        load(4, c_in, c, h).start()
        return 0

    def lanes(h):
        return pl.ds(pl.multiple_of(h * HD, HD), HD)

    barrier = pltpu.get_barrier_semaphore()
    for p in ctx_peers:
        pl.semaphore_signal(barrier, inc=1, device_id={"ctx": p}, device_id_type=MESH)
    for p in tp_peers:
        pl.semaphore_signal(barrier, inc=1, device_id={"tp": p}, device_id_type=MESH)
    pl.semaphore_signal(barrier, inc=1, device_id={"dp": partner}, device_id_type=MESH)
    slopes_copy = pltpu.make_async_copy(slopes_in, slopes, small_sem.at[0])
    gain_copy_in = pltpu.make_async_copy(gain_in, gain_ref, small_sem.at[1])
    slopes_copy.start()
    lax.fori_loop(0, PER, load_kv, 0)
    lax.fori_loop(PER, HEADS_HERE, load_kv, 0)
    gain_copy_in.start()
    lax.fori_loop(0, HEADS_HERE, load_rest, 0)
    slopes_copy.wait()

    position = lax.broadcasted_iota(jnp.int32, (BLOCK, HD), 0).astype(F32)
    along = lax.broadcasted_iota(jnp.int32, (1, BLOCK), 1).astype(F32)

    def exchange(src, dst, send, recv, n, p):
        return pltpu.make_async_remote_copy(
            src_ref=src.at[n, p],
            dst_ref=dst.at[n, me],
            send_sem=send.at[n],
            recv_sem=recv.at[n],
            device_id={"ctx": p},
            device_id_type=MESH,
        )

    def send_all(src, dst, send, recv, n):
        for p in ctx_peers:
            exchange(src, dst, send, recv, n, p).start()
        dst[n, me] = src[n, me]

    def waiter(src, dst, send, recv, n):
        return pltpu.make_async_remote_copy(
            src_ref=src.at[n, pl.ds(0, CTX - 1)],
            dst_ref=dst.at[n, pl.ds(0, CTX - 1)],
            send_sem=send.at[n],
            recv_sem=recv.at[n],
            device_id={"ctx": ctx_peers[0]},
            device_id_type=MESH,
        )

    def scan(d, n, reverse):
        waiter(u.at[d], r1.at[d], send1.at[d], recv1.at[d], n).wait_recv()
        fade = jnp.concatenate(
            [
                jnp.exp(jnp.full((PART, HD), -slopes[n * PER + i] * BLOCK, F32))
                for i in range(PER)
            ],
            axis=0,
        )
        total = jnp.zeros((ROWS, HD), F32)
        for b in reversed(range(CTX)) if reverse else range(CTX):
            s2[d, n, b] = total
            total = fade * total + r1[d, n, b]
        send_all(s2.at[d], r2.at[d], send2.at[d], recv2.at[d], n)

    def state(d, n, i):
        return r2[d, n, :, i * PART : (i + 1) * PART, :].reshape(HD, HD).astype(BF16)

    def put(d, n, i, value):
        u[d, n, :, i * PART : (i + 1) * PART, :] = value.reshape(CTX, PART, HD)

    def summary(n):
        for i in range(PER):
            h = n * PER + i
            before[h] = jnp.exp(-slopes[h] * (BLOCK - 1.0 - position))
        for i in range(PER):
            h = n * PER + i
            load(1, k_in, k, h).wait()
            load(2, v_in, v, h).wait()
            scaled_keys = (k[h].astype(F32) * before[h]).astype(BF16)
            put(0, n, i, dot(v[h], scaled_keys, TN))

    def first(n, _):
        summary(n)
        send_all(u.at[0], r1.at[0], send1.at[0], recv1.at[0], n)
        return 0

    summary(0)
    pl.semaphore_wait(barrier, CTX - 1 + TP - 1 + 1)
    send_all(u.at[0], r1.at[0], send1.at[0], recv1.at[0], 0)
    lax.fori_loop(1, CHUNKS, first, 0)

    distance = (
        lax.broadcasted_iota(jnp.int32, (HALF, HALF), 0)
        - lax.broadcasted_iota(jnp.int32, (HALF, HALF), 1)
    ).astype(F32)

    def inside(h, _):
        load(0, q_in, q, h).wait()
        load(3, g_in, g, h).wait()
        load(4, c_in, c, h).wait()
        rate = slopes[h]
        near = jnp.where(distance >= 0.0, jnp.exp(-rate * jnp.maximum(distance, 0.0)), 0.0)
        far = jnp.exp(-rate * (distance + HALF))
        w_near[h] = near
        w_far[h] = far
        top, bottom = q[h, :HALF], q[h, HALF:]
        k_top, k_bottom = k[h, :HALF], k[h, HALF:]
        masked[h, 0] = (dot(top, k_top, NT) * near).astype(BF16)
        masked[h, 1] = (dot(bottom, k_top, NT) * far).astype(BF16)
        masked[h, 2] = (dot(bottom, k_bottom, NT) * near).astype(BF16)
        att_t[h, :, :HALF] = dot(masked[h, 0], v[h, :HALF], NN).T
        att_t[h, :, HALF:] = (
            dot(masked[h, 1], v[h, :HALF], NN) + dot(masked[h, 2], v[h, HALF:], NN)
        ).T
        weight = jnp.exp(-rate * (position + 1.0))
        after[h] = weight
        qs[h] = (q[h].astype(F32) * weight).astype(BF16)
        q_t[h] = q[h].T
        gated = 1.0 / (1.0 + jnp.exp(-g[h].astype(F32)))
        normed = c[h].astype(F32) * gated
        nrm[h] = normed
        sca_t[h] = (normed * gain_ref[pl.ds(h, 1), :]).T
        omg[h] = 1.0 - gated
        return 0

    def scan_forward(n, _):
        scan(0, n, False)
        return 0

    gain_copy_in.wait()
    lax.fori_loop(0, HEADS_HERE // 2, inside, 0)
    lax.fori_loop(0, CHUNKS, scan_forward, 0)
    lax.fori_loop(HEADS_HERE // 2, HEADS_HERE, inside, 0)

    sums[...] = jnp.zeros_like(sums)

    def attend(n, _):
        waiter(s2.at[0], r2.at[0], send2.at[0], recv2.at[0], n).wait_recv()
        for i in range(PER):
            h = n * PER + i
            memory = state(0, n, i)
            mem[h] = memory
            fade = jnp.exp(-slopes[h] * (along + 1.0))
            attended = att_t[h] + fade * dot(memory, q_t[h], NN)
            att_t[h] = attended
            sums[0] += jnp.sum((attended * attended).reshape(HD // 8, 8, BLOCK), axis=0)
            sums[1] += jnp.sum((sca_t[h] * attended).reshape(HD // 8, 8, BLOCK), axis=0)
        return 0

    lax.fori_loop(0, CHUNKS, attend, 0)
    rows = []
    for n in range(2):
        row = jnp.sum(sums[n], axis=0, keepdims=True)
        rows += [row[:, t * HD : (t + 1) * HD] for t in range(BLOCK // HD)]
    zsend[...] = jnp.concatenate(rows, axis=0)

    def tp_copy(i):
        return pltpu.make_async_remote_copy(
            src_ref=zsend,
            dst_ref=zrecv.at[my_tp],
            send_sem=zs_sem.at[i],
            recv_sem=zr_sem.at[i],
            device_id={"tp": tp_peers[i]},
            device_id_type=MESH,
        )

    for i in range(TP - 1):
        tp_copy(i).start()
    zrecv[my_tp] = zsend[...]
    for i in range(TP - 1):
        tp_copy(i).wait_recv()
    totals = zrecv[0]
    for i in range(1, TP):
        totals = totals + zrecv[i]
    radius = lax.rsqrt(totals[:4] / FEATURES + EPSILON)
    cross = radius * radius * radius * totals[4:] / FEATURES
    stats[0] = jnp.concatenate([radius[t : t + 1] for t in range(4)], axis=1)
    stats[1] = jnp.concatenate([cross[t : t + 1] for t in range(4)], axis=1)

    def second(n, _):
        for i in range(PER):
            h = n * PER + i
            gradient = (stats[0] * sca_t[h] - stats[1] * att_t[h]).astype(BF16)
            ga_t[h] = gradient
            put(1, n, i, dot(gradient, qs[h], NN))
        send_all(u.at[1], r1.at[1], send1.at[1], recv1.at[1], n)
        return 0

    lax.fori_loop(0, CHUNKS, second, 0)

    for t in range(BLOCK // HD):
        column = stats[0, :, t * HD : (t + 1) * HD]
        rcol[t * HD : (t + 1) * HD, :] = jnp.broadcast_to(column, (HD, HD)).T

    def gate(h, _):
        ga[h] = ga_t[h].T
        common = nrm[h] * att_t[h].T * rcol[...]
        gsend[pl.ds(h, 1), :] = jnp.sum(common, axis=0, keepdims=True)
        dg[:, lanes(h)] = (common * gain_ref[pl.ds(h, 1), :] * omg[h]).astype(BF16)
        return 0

    lax.fori_loop(0, HEADS_HERE, gate, 0)
    pair = pltpu.make_async_remote_copy(
        src_ref=gsend,
        dst_ref=gpart,
        send_sem=g_sem.at[0],
        recv_sem=g_sem.at[1],
        device_id={"dp": partner},
        device_id_type=MESH,
    )
    pair.start()

    def backward(h, _):
        gradient = ga[h]
        g_top, g_bottom = ga[h, :HALF], ga[h, HALF:]
        v_top, v_bottom = v[h, :HALF], v[h, HALF:]
        near, far = w_near[h], w_far[h]
        m0 = (dot(g_top, v_top, NT) * near).astype(BF16)
        m1 = (dot(g_bottom, v_top, NT) * far).astype(BF16)
        m2 = (dot(g_bottom, v_bottom, NT) * near).astype(BF16)
        gm[0] = m0
        gm[1] = m1
        gm[2] = m2
        k_top, k_bottom = k[h, :HALF], k[h, HALF:]
        carried = after[h] * dot(gradient, mem[h], NN)
        dq[:HALF, lanes(h)] = (dot(gm[0], k_top, NN) + carried[:HALF]).astype(BF16)
        dq[HALF:, lanes(h)] = (
            dot(gm[1], k_top, NN) + dot(gm[2], k_bottom, NN) + carried[HALF:]
        ).astype(BF16)
        dki[h, :HALF] = dot(gm[0], q[h, :HALF], TN) + dot(gm[1], q[h, HALF:], TN)
        dki[h, HALF:] = dot(gm[2], q[h, HALF:], TN)
        dvi[h, :HALF] = dot(masked[h, 0], g_top, TN) + dot(masked[h, 1], g_bottom, TN)
        dvi[h, HALF:] = dot(masked[h, 2], g_bottom, TN)
        return 0

    def scan_backward(n, _):
        scan(1, n, True)
        return 0

    lax.fori_loop(0, 4, backward, 0)
    pair.wait_recv()
    gsum[0] = gsend[...] + gpart[...]

    def gain_copy(stage, o):
        place = lax.rem((me_x, me_y)[stage] + o, 4)
        return pltpu.make_async_remote_copy(
            src_ref=gsum.at[stage],
            dst_ref=grecv.at[stage, (me_x, me_y)[stage]],
            send_sem=g_sem.at[2 + 2 * stage],
            recv_sem=g_sem.at[3 + 2 * stage],
            device_id={"ctx": (me_y * CTX_X + place, place * CTX_X + me_x)[stage]},
            device_id_type=MESH,
        )

    def gain_start(stage):
        for o in (2, 1, 3):
            gain_copy(stage, o).start()
        grecv[stage, (me_x, me_y)[stage]] = gsum[stage]

    def gain_all(stage):
        return pltpu.make_async_remote_copy(
            src_ref=grecv.at[stage, pl.ds(0, 3)],
            dst_ref=grecv.at[stage, pl.ds(0, 3)],
            send_sem=g_sem.at[2 + 2 * stage],
            recv_sem=g_sem.at[3 + 2 * stage],
            device_id={"ctx": ctx_peers[0]},
            device_id_type=MESH,
        )

    gain_start(0)
    lax.fori_loop(0, CHUNKS, scan_backward, 0)
    gain_all(0).wait_recv()
    gsum[1] = grecv[0, 0] + grecv[0, 1] + grecv[0, 2] + grecv[0, 3]
    gain_start(1)
    lax.fori_loop(4, HEADS_HERE, backward, 0)

    def sent(n, _):
        waiter(u.at[0], r1.at[0], send1.at[0], recv1.at[0], n).wait_send()
        waiter(s2.at[0], r2.at[0], send2.at[0], recv2.at[0], n).wait_send()
        waiter(u.at[1], r1.at[1], send1.at[1], recv1.at[1], n).wait_send()
        return 0

    lax.fori_loop(0, CHUNKS, sent, 0)
    for i in range(TP - 1):
        tp_copy(i).wait_send()
    pair.wait_send()

    def finish(n, _):
        waiter(s2.at[1], r2.at[1], send2.at[1], recv2.at[1], n).wait_recv()
        for i in range(PER):
            h = n * PER + i
            recalled = state(1, n, i)
            dk[:, lanes(h)] = (dki[h] + before[h] * dot(v[h], recalled, NN)).astype(BF16)
            dv[:, lanes(h)] = (dvi[h] + before[h] * dot(k[h], recalled, NT)).astype(BF16)
        return 0

    lax.fori_loop(0, CHUNKS, finish, 0)

    gain_all(1).wait_recv()
    gain_out[...] = grecv[1, 0] + grecv[1, 1] + grecv[1, 2] + grecv[1, 3]
    gain_all(0).wait_send()
    gain_all(1).wait_send()

    def drain(n, _):
        waiter(s2.at[1], r2.at[1], send2.at[1], recv2.at[1], n).wait_send()
        return 0

    lax.fori_loop(0, CHUNKS, drain, 0)


def place(dq_in, dk_in, dv_in, dg_in, gain_in, dq, dk, dv, dg, gain, sem, gain_sem):
    pairs = ((dq_in, dq), (dk_in, dk), (dv_in, dv), (dg_in, dg))
    copies = [
        pltpu.make_async_copy(
            src.at[pl.ds(i * PIECE, PIECE)], dst.at[0, pl.ds(i * PIECE, PIECE)], sem.at[n, i]
        )
        for i in range(BLOCK // PIECE)
        for n, (src, dst) in enumerate(pairs)
    ]
    copies.append(pltpu.make_async_copy(gain_in, gain, gain_sem))
    for copy in copies:
        copy.start()
    for copy in copies:
        copy.wait()


def per_device(queries, keys, values, gate, cotangent, gain, slopes):
    whole = jax.ShapeDtypeStruct((1, BLOCK, HEADS_HERE * HD), BF16)
    flat = pltpu.VMEM((BLOCK, HEADS_HERE * HD), BF16)
    heads16 = pltpu.VMEM((HEADS_HERE, BLOCK, HD), BF16)
    heads32 = pltpu.VMEM((HEADS_HERE, BLOCK, HD), F32)
    heads16_t = pltpu.VMEM((HEADS_HERE, HD, BLOCK), BF16)
    heads32_t = pltpu.VMEM((HEADS_HERE, HD, BLOCK), F32)
    travel = pltpu.VMEM((2, CHUNKS, CTX, ROWS, HD), F32)
    tile = pltpu.VMEM((HEADS_HERE, HD), F32)
    dma = pltpu.SemaphoreType.DMA
    scratch = (
        [pltpu.SMEM((HEADS_HERE,), F32), tile]
        + [heads16] * 5
        + [
            heads32,
            heads32,
            pltpu.VMEM((HEADS_HERE, 3, HALF, HALF), BF16),
            pltpu.VMEM((HEADS_HERE, HALF, HALF), F32),
            pltpu.VMEM((HEADS_HERE, HALF, HALF), F32),
            heads32_t,
            heads32_t,
            heads32,
            heads32,
            heads16,
            heads16_t,
            heads16_t,
            heads16,
            pltpu.VMEM((HEADS_HERE, HD, HD), BF16),
            pltpu.VMEM((3, HALF, HALF), BF16),
            heads32,
            heads32,
        ]
        + [
            pltpu.VMEM((2, 8, BLOCK), F32),
            pltpu.VMEM((2, 1, BLOCK), F32),
            pltpu.VMEM((BLOCK, HD), F32),
        ]
        + [travel] * 4
        + [
            tile,
            pltpu.VMEM((TP, 8, HD), F32),
            tile,
            tile,
            pltpu.VMEM((2, HEADS_HERE, HD), F32),
            pltpu.VMEM((2, 4, HEADS_HERE, HD), F32),
            dma((2,)),
            dma((5, HEADS_HERE)),
        ]
        + [dma((2, CHUNKS))] * 4
        + [dma((TP - 1,)), dma((TP - 1,)), dma((6,))]
    )
    anywhere = pl.BlockSpec(memory_space=pl.ANY)
    in_hbm = pl.BlockSpec(memory_space=pltpu.HBM)
    in_vmem = pl.BlockSpec(memory_space=pltpu.VMEM)
    flops = HEADS_HERE * BLOCK * HD * 2 * (6 * BLOCK * 3 // 4 + 6 * HD)
    whole_inputs = [
        pltpu.with_memory_space_constraint(x, pltpu.HBM)
        for x in (
            slopes, queries, keys, values, gate, cotangent, gain.reshape(HEADS_HERE, HD)
        )
    ]
    results = pl.pallas_call(
        kernel,
        out_shape=(flat, flat, flat, flat, tile),
        in_specs=[in_hbm] * 7,
        out_specs=(in_vmem,) * 5,
        scratch_shapes=scratch,
        compiler_params=pltpu.CompilerParams(
            collective_id=0, has_side_effects=True, vmem_limit_bytes=44 << 20
        ),
        cost_estimate=pl.CostEstimate(
            flops=flops, bytes_accessed=5 << 20, transcendentals=HEADS_HERE * BLOCK * BLOCK
        ),
        name="lightning_backward",
    )(*whole_inputs)
    results = [pltpu.with_memory_space_constraint(x, pltpu.VMEM) for x in results]
    dq, dk, dv, dg, total = pl.pallas_call(
        place,
        out_shape=(whole, whole, whole, whole, jax.ShapeDtypeStruct((HEADS_HERE, HD), F32)),
        in_specs=[in_vmem] * 5,
        out_specs=(anywhere,) * 5,
        scratch_shapes=[dma((4, BLOCK // PIECE)), dma],
        compiler_params=pltpu.CompilerParams(vmem_limit_bytes=2 << 20),
        cost_estimate=pl.CostEstimate(flops=0, bytes_accessed=8 << 20, transcendentals=0),
        name="place_results",
    )(*results)
    return dq, dk, dv, dg, total.reshape(HEADS_HERE * HD)


def solution(mesh):
    wide = P("dp", "ctx", "tp")
    return jax.shard_map(
        per_device,
        mesh=mesh,
        in_specs=(wide, wide, wide, wide, wide, P("tp"), P("tp")),
        out_specs=(wide, wide, wide, wide, P("tp")),
        check_vma=False,
    )
```
